32 devices in a mesh: grp: 2 (over x), lat: 8 (over z, y), chan: 2 (over core).
Axes of the slice: x: 2, y: 2, z: 4, core: 2. Of those that a mesh axis runs over, the one named last changes fastest.
Arguments:
- state_in: bfloat16 [32, 1440, 512], P(('grp', 'lat'), None, 'chan'), parts along dimension 0, may hold values from -6 to 6
- basis_blocks: bfloat16 [16, 5, 80, 3, 4, 80], P('lat'), may hold values from -0.1875 to 0.1875
- block_start: int32 [16, 3], P('lat'), may hold values from 0 to 17
- block_count: int32 [16, 3], P('lat'), may hold values from 1 to 4, as said below
- mix_weight: bfloat16 [5, 512, 512], P(None, 'chan'), may hold values from -0.125 to 0.125
- up_weight: bfloat16 [512, 1024], P(None, 'chan'), may hold values from -0.25 to 0.25
- down_weight: bfloat16 [1024, 512], P('chan'), may hold values from -0.1875 to 0.1875
Outputs:
- state_out: bfloat16 [32, 1440, 512], P(('grp', 'lat'), None, 'chan'), parts along dimension 0
The draws below stay inside these ranges and needn't reach their ends.
There are 2 independent parts, one for each index of `grp`. The reference program is written for one: setup_inputs(seed, part) draws one part's arguments, and reference() takes and returns one part's arrays. A program takes and returns all parts, laid end to end along the dimension named above; an argument that names none is the same for every part. Nothing has to cross between parts.
Inputs may be any that keep to these rules, and one draw needn't show every extreme that they name: `block_count`: the count of row i and tap t is min(4, 1 + 3 * (16 - i) * (16 - i) // 256 + e), e being 0 or 1 drawn for each row and tap.
All inputs are finite; a program needn't handle non-finite values.
Results may differ from the reference program's by a relative error of at most 0.0049.
Values may be sent and summed in bfloat16 or wider, within the bound.
No kernel may reach another device: no remote copies, remote signals or barrier semaphores. Data moves between devices by JAX's collectives and lax.ppermute only.
A program may use at most 128 MiB of HBM per device.

```python
import jax
import jax.numpy as jnp
from jax import lax

NLON = 1440
C = 512
FF = 1024
K = 5
BL = 80
NB = 4
NLAT = 16
NQ = 18


def draw_block_count(key, part):
    key = jax.random.fold_in(key, 7)
    row_index = jnp.arange(NLAT, dtype=jnp.int32)[:, None]
    distance = NLAT - row_index
    baseline = 1 + (NB - 1) * distance * distance // (NLAT * NLAT)
    jitter = jax.random.randint(key, (NLAT, 3), 0, 2, dtype=jnp.int32)
    return jnp.minimum(baseline + jitter, NB).astype(jnp.int32)


def set_ends(values, rng, least, largest):
    longest = values.shape.index(max(values.shape))
    spots = []
    for shift in (0, 1):
        where = [jax.random.randint(jax.random.fold_in(rng, axis), (), 0, length) for axis, length in enumerate(values.shape)]
        where[longest] = (where[longest] + shift) % values.shape[longest]
        spots.append(tuple(where))
    return values.at[spots[0]].set(least).at[spots[1]].set(largest)


def levels(stream_key, shape, split, low, top_value):
    loudness, own = 1.0, jax.random.fold_in(stream_key, 6)
    for position, shards_of in split:
        heights = jnp.exp(jax.random.uniform(jax.random.fold_in(own, position), (shards_of,), jnp.float32, low / len(split), top_value / len(split)))
        loudness = loudness * jnp.repeat(heights, shape[position] // shards_of).reshape([-1 if axis == position else 1 for axis in range(len(shape))])
    return loudness


def bell_draw(key, dims, scale, reach, cuts=(), held_as=jnp.bfloat16):
    array = scale * jax.random.normal(key, dims, jnp.float32)
    if cuts:
        array = array * levels(key, dims, cuts, -0.22, 0.18)
    return jnp.clip(array, -reach, reach).astype(held_as)


def setup_inputs(seed: int = 0, part: int = 0) -> dict:
    splits = jax.random.split(jax.random.key(seed), 8)
    part_splits = jax.random.split(jax.random.fold_in(splits[7], part), 8)
    state_in = bell_draw(part_splits[0], (NLAT, NLON, C), 1.0, 6.0, ((0, 8), (2, 2)))
    basis_blocks = bell_draw(splits[1], (NLAT, K, BL, 3, NB, BL), (3 * NB * BL) ** -0.5, 0.1875, ((0, 8),))
    block_start = set_ends(jax.random.randint(splits[2], (NLAT, 3), 0, NQ), jax.random.fold_in(splits[2], 1), 0, NQ - 1).astype(jnp.int32)
    block_count = draw_block_count(jax.random.fold_in(splits[7], 71), part)
    mix_weight = bell_draw(splits[4], (K, C, C), (K * C) ** -0.5, 0.125, ((1, 2),))
    up_weight = bell_draw(splits[5], (C, FF), C ** -0.5, 0.25, ((1, 2),))
    down_weight = bell_draw(splits[6], (FF, C), FF ** -0.5, 0.1875, ((0, 2),))
    return {"state_in": state_in, "basis_blocks": basis_blocks, "block_start": block_start, "block_count": block_count, "mix_weight": mix_weight, "up_weight": up_weight, "down_weight": down_weight}


def reference(state_in, basis_blocks, block_start, block_count, mix_weight, up_weight, down_weight):
    lat_rows, lon_cells, channels = state_in.shape
    basis_count = basis_blocks.shape[1]
    block_width = basis_blocks.shape[2]
    block_most = basis_blocks.shape[4]
    lon_blocks = lon_cells // block_width
    zero_row = jnp.zeros((1, lon_cells, channels), state_in.dtype)
    padded = jnp.concatenate([zero_row, state_in, zero_row], 0)

    def one_row(row_index):
        window = lax.dynamic_slice_in_dim(padded, row_index, 3, 0).reshape(3, lon_blocks, block_width, channels)
        filters_row = basis_blocks[row_index]
        counts_row = block_count[row_index]
        starts_row = block_start[row_index]
        pieces = []
        for lat_tap in range(3):
            for block_index in range(block_most):
                pieces.append(jnp.roll(window[lat_tap], -(starts_row[lat_tap] + block_index), axis=0))
        stacked = jnp.stack(pieces, 1).reshape(lon_blocks, 3 * block_most * block_width, channels)
        keep = jnp.arange(block_most, dtype=jnp.int32)[None, :] < counts_row[:, None]
        weights = jnp.where(keep[None, None, :, :, None], filters_row.astype(jnp.float32), 0.0)
        weights = weights.reshape(basis_count, block_width, 3 * block_most * block_width)
        result = jnp.einsum("kaz,qzc->kqac", weights, stacked.astype(jnp.float32))
        conv = lax.optimization_barrier(result.reshape(basis_count, lon_cells, channels).astype(jnp.bfloat16))
        mixed = jnp.einsum("kjc,kco->jo", conv.astype(jnp.float32), mix_weight.astype(jnp.float32))
        state = state_in[row_index].astype(jnp.float32) + mixed
        rounded = state.astype(jnp.bfloat16)
        hidden = jax.nn.gelu(jnp.dot(rounded, up_weight, preferred_element_type=jnp.float32), approximate=False).astype(jnp.bfloat16)
        feed = jnp.dot(hidden, down_weight, preferred_element_type=jnp.float32)
        return (state + feed).astype(jnp.bfloat16)

    return lax.map(one_row, jnp.arange(lat_rows, dtype=jnp.int32))
```

```python
import functools

import jax
import jax.numpy as jnp
from jax import lax
from jax.experimental import pallas as pl
from jax.experimental.pallas import tpu as pltpu
from jax.sharding import PartitionSpec as P

GROUP = 6


def fill_window(window, halves, width, cells):
    most = window.shape[0] - cells
    for index, half in enumerate(halves):
        lanes = slice(index * width, (index + 1) * width)
        window[:cells, lanes] = half
        window[cells:, lanes] = half[:most]


def filter_group(group, block_width, basis_count, channels, weights, windows, starts, lon_blocks, conv):
    most = (windows[0].shape[0] // block_width) - lon_blocks + 1
    for slot in range(GROUP):
        block = group * GROUP + slot
        parts = []
        for window, start in zip(windows, starts):
            first = lax.rem(block + start, lon_blocks) * block_width
            first = pl.multiple_of(first, block_width)
            parts.append(window[pl.ds(first, most * block_width), :])
        cells = parts[0] if len(parts) == 1 else jnp.concatenate(parts, axis=0)
        result = jnp.dot(weights, cells, preferred_element_type=jnp.float32).astype(jnp.bfloat16)
        for basis in range(basis_count):
            conv[slot * block_width : (slot + 1) * block_width, basis * channels : (basis + 1) * channels] = (
                result[basis * block_width : (basis + 1) * block_width]
            )


def local_kernel(
    scalars, own, other, weights, mix, result, window0, window1, conv,
    *, block_width, basis_count, lon_blocks,
):
    group = pl.program_id(0)
    cells, width = own.shape[1], own.shape[2]

    @pl.when(group == 0)
    def _():
        for row, window in enumerate((window0, window1)):
            fill_window(window, (own[row], other[row]), width, cells)

    filter_group(
        group, block_width, basis_count, 2 * width, weights[...], (window0, window1),
        (scalars[0], scalars[1]), lon_blocks, conv,
    )
    mixed = jnp.dot(conv[...], mix[...], preferred_element_type=jnp.float32)
    core = scalars[3]
    rows = pl.ds(pl.multiple_of(group * GROUP * block_width, GROUP * block_width), GROUP * block_width)
    near = own[core, rows, :].astype(jnp.float32)
    far = other[core, rows, :].astype(jnp.float32)
    low = jnp.where(core == 0, near, far)
    high = jnp.where(core == 0, far, near)
    result[:, :width] = mixed[:, :width] + low
    result[:, width:] = mixed[:, width:] + high


def gelu(x):
    return 0.5 * x * (1.0 + lax.erf(x * 0.7071067811865476))


def tail_kernel(
    scalars, own, other, weights, mix, partial, up, down, keep, send, window, conv,
    *, block_width, basis_count, lon_blocks,
):
    group = pl.program_id(0)
    cells, width = own.shape

    @pl.when(group == 0)
    def _():
        fill_window(window, (own[...], other[...]), width, cells)

    filter_group(
        group, block_width, basis_count, 2 * width, weights[...], (window,), (scalars[2],), lon_blocks, conv
    )
    state = partial[...] + jnp.dot(conv[...], mix[...], preferred_element_type=jnp.float32)
    rounded = state.astype(jnp.bfloat16)
    hidden = gelu(jnp.dot(rounded, up[...], preferred_element_type=jnp.float32)).astype(jnp.bfloat16)
    feed = jnp.dot(hidden, down[...], preferred_element_type=jnp.float32)
    total = (state + feed).astype(jnp.bfloat16)
    low, high = total[:, :width], total[:, width:]
    core = scalars[3]
    keep[...] = jnp.where(core == 0, low, high)
    send[...] = jnp.where(core == 0, high, low)


def whole(shape):
    return pl.BlockSpec(shape, lambda *_: (0,) * len(shape), pipeline_mode=pl.Buffered(1))


def per_device(
    state_in, basis_blocks, block_start, block_count, mix_weight, up_weight, down_weight
):
    core = lax.axis_index("chan")
    bands = lax.axis_size("lat")
    basis_count, block_width, taps, block_most = basis_blocks.shape[1:5]
    cells, width = state_in.shape[1:]
    channels = mix_weight.shape[2]
    lon_blocks = cells // block_width
    swap = [(0, 1), (1, 0)]
    pairs = []
    for band in range(bands - 1):
        pairs += [(2 * band + 1, 2 * band + 2), (2 * band + 2, 2 * band + 1)]

    halo_other = lax.ppermute(jnp.where(core == 0, state_in[0], state_in[1]), ("lat", "chan"), pairs)
    other = lax.ppermute(state_in, "chan", swap)
    halo_own = lax.ppermute(jnp.where(core == 0, other[0], other[1]), ("lat", "chan"), pairs)
    mix = jnp.concatenate([mix_weight, lax.ppermute(mix_weight, "chan", swap)], 1)
    mix = mix.reshape(basis_count * channels, channels)
    up = jnp.concatenate([up_weight, lax.ppermute(up_weight, "chan", swap)], 1)
    down = jnp.concatenate([down_weight, lax.ppermute(down_weight, "chan", swap)], 0)

    counts = block_count[core]
    starts = block_start[core]
    kept = jnp.arange(block_most, dtype=jnp.int32)[None, :] < counts[:, None]
    filters = jnp.where(kept[None, None, :, :, None], basis_blocks[core], 0)
    filters = filters.reshape(basis_count * block_width, taps, block_most * block_width)
    near = lax.dynamic_slice_in_dim(filters, 1 - core, 2, 1)
    near = near.reshape(basis_count * block_width, 2 * block_most * block_width)
    edge = lax.dynamic_index_in_dim(filters, 2 * core, 1, keepdims=False)
    scalars = jnp.stack([starts[1 - core], starts[2 - core], starts[2 * core], core])

    rows = GROUP * block_width
    sizes = dict(block_width=block_width, basis_count=basis_count, lon_blocks=lon_blocks)
    window = pltpu.VMEM((cells + (block_most - 1) * block_width, channels), jnp.bfloat16)
    conv = pltpu.VMEM((rows, basis_count * channels), jnp.bfloat16)
    params = pltpu.CompilerParams(vmem_limit_bytes=40 * 1024 * 1024)
    mix_flops = 2 * cells * basis_count * channels * channels

    def conv_flops(depth):
        return 2 * basis_count * cells * depth * block_most * block_width * channels

    partial = pl.pallas_call(
        functools.partial(local_kernel, **sizes),
        out_shape=jax.ShapeDtypeStruct((cells, channels), jnp.float32),
        grid_spec=pltpu.PrefetchScalarGridSpec(
            num_scalar_prefetch=1,
            grid=(cells // rows,),
            in_specs=[whole(state_in.shape), whole(other.shape), whole(near.shape), whole(mix.shape)],
            out_specs=pl.BlockSpec((rows, channels), lambda i, _: (i, 0)),
            scratch_shapes=[window, window, conv],
        ),
        compiler_params=params,
        cost_estimate=pl.CostEstimate(
            flops=mix_flops + conv_flops(2), bytes_accessed=10_000_000, transcendentals=0
        ),
        name="local_taps",
    )(scalars, state_in, other, near, mix)

    half = jax.ShapeDtypeStruct((cells, width), jnp.bfloat16)
    keep, send = pl.pallas_call(
        functools.partial(tail_kernel, **sizes),
        out_shape=(half, half),
        grid_spec=pltpu.PrefetchScalarGridSpec(
            num_scalar_prefetch=1,
            grid=(cells // rows,),
            in_specs=[
                whole(halo_own.shape), whole(halo_other.shape), whole(edge.shape), whole(mix.shape),
                pl.BlockSpec((rows, channels), lambda i, _: (i, 0)),
                whole(up.shape), whole(down.shape),
            ],
            out_specs=[pl.BlockSpec((rows, width), lambda i, _: (i, 0))] * 2,
            scratch_shapes=[window, conv],
        ),
        compiler_params=params,
        cost_estimate=pl.CostEstimate(
            flops=mix_flops + conv_flops(1) + 8 * cells * channels * channels,
            bytes_accessed=10_000_000, transcendentals=cells * up.shape[1],
        ),
        name="edge_tap_and_feed",
    )(scalars, halo_own, halo_other, edge, mix, partial, up, down)

    received = lax.ppermute(send, "chan", swap)
    first = jnp.where(core == 0, keep, received)
    second = jnp.where(core == 0, received, keep)
    return jnp.stack([first, second])


def solution(mesh):
    placed = (
        P(("grp", "lat"), None, "chan"),
        P("lat", None, None, None, None, None),
        P("lat", None),
        P("lat", None),
        P(None, "chan", None),
        P(None, "chan"),
        P("chan", None),
    )
    return jax.shard_map(
        per_device,
        mesh=mesh,
        in_specs=placed,
        out_specs=P(("grp", "lat"), None, "chan"),
        check_vma=False,
    )
```

```python
import functools

import jax
import jax.numpy as jnp
from jax import lax
from jax.experimental import pallas as pl
from jax.experimental.pallas import tpu as pltpu
from jax.sharding import PartitionSpec as P

GROUP = 9
FIRST = 8
TILE = 16


def start_all(copies):
    for copy in copies:
        copy.start()
    return copies


def wait_all(copies):
    for copy in copies:
        copy.wait()


def halo_start(block_start, core):
    return block_start[core, 2 * core]


def block_rows(block, block_width, blocks=1):
    return pl.ds(pl.multiple_of(block * block_width, block_width), blocks * block_width)


def home_block(place, start, lon_blocks):
    return lax.rem(place + lon_blocks - start, lon_blocks)


def spread_filters(basis, counts, core, filters, block_most):
    rows_out, taps, width = filters.shape[1], filters.shape[0], basis.shape[1]
    pieces = taps * block_most
    size = TILE * pieces
    row = lax.broadcasted_iota(jnp.int32, (size, size), 0)
    column = lax.broadcasted_iota(jnp.int32, (size, size), 1)
    order = (column == lax.rem(row, TILE) * pieces + row // TILE).astype(jnp.float32).astype(jnp.bfloat16)
    for tile in range(rows_out // TILE):
        sorted_rows = jnp.dot(
            order, basis[tile * size : (tile + 1) * size, :], preferred_element_type=jnp.float32
        ).astype(jnp.bfloat16)
        for tap in range(taps):
            for block in range(block_most):
                at = (tap * block_most + block) * TILE
                piece = sorted_rows[at : at + TILE]
                filters[tap, tile * TILE : (tile + 1) * TILE, block * width : (block + 1) * width] = (
                    jnp.where(block < counts[core, tap], piece, jnp.zeros_like(piece))
                )


def filter_kernel(block_count, basis_from, near, edge, basis, filters, sem, *, block_most):
    core = lax.axis_index("chan")
    rows = basis.shape[0]
    depth = filters.shape[2]
    copy = pltpu.make_async_copy(
        basis_from.at[pl.ds(pl.multiple_of(core * rows, rows), rows), :], basis, sem
    )
    copy.start()
    copy.wait()
    spread_filters(basis, block_count, core, filters, block_most)
    near[:, :depth] = filters[1 - core]
    near[:, depth:] = filters[2 - core]
    edge[...] = filters[2 * core]


def local_kernel(
    block_start, near, own, other, conv_own, conv_other, residual, window0, window1,
    *, lon_blocks, block_width, block_most,
):
    core = lax.axis_index("chan")
    cells, width = own.shape[1:]
    for row, window in enumerate((window0, window1)):
        extra = window.shape[0] - cells
        for half, source in enumerate((own, other)):
            lanes = slice(half * width, (half + 1) * width)
            window[:cells, lanes] = source[row]
            window[cells:, lanes] = source[row, :extra]
    start = halo_start(block_start, core)
    for place in range(lon_blocks):
        source = block_rows(home_block(place, start, lon_blocks), block_width)
        target = slice(place * block_width, (place + 1) * block_width)
        mine = own[core, source, :].astype(jnp.float32)
        theirs = other[core, source, :].astype(jnp.float32)
        residual[target, :width] = jnp.where(core == 0, mine, theirs)
        residual[target, width:] = jnp.where(core == 0, theirs, mine)
    starts = (block_start[core, 1 - core], block_start[core, 2 - core])

    def group_step(group, carry):
        for slot in range(GROUP):
            block = group * GROUP + slot
            parts = []
            for window, start in zip((window0, window1), starts):
                place = lax.rem(block + start, lon_blocks)
                parts.append(window[block_rows(place, block_width, block_most), :])
            result = jnp.dot(near[...], jnp.concatenate(parts, axis=0), preferred_element_type=jnp.float32)
            conv_own[block] = result[:, :width]
            conv_other[block] = result[:, width:]
        return carry

    lax.fori_loop(0, lon_blocks // GROUP, group_step, 0)


def halo_conv(first, places, start, lon_blocks, block_width, window, edge_filter, conv_local, conv):
    depth = edge_filter.shape[1]
    width = window.shape[1]
    for slot in range(places):
        home = home_block(first + slot, start, lon_blocks)
        result = conv_local[home] + jnp.dot(
            edge_filter[...], window[slot * block_width : slot * block_width + depth, :],
            preferred_element_type=jnp.float32,
        )
        rounded = result.astype(jnp.bfloat16)
        for basis in range(edge_filter.shape[0] // block_width):
            conv[
                slot * block_width : (slot + 1) * block_width, basis * width : (basis + 1) * width
            ] = rounded[basis * block_width : (basis + 1) * block_width]


def first_half_kernel(
    block_start, half, edge_filter, conv_local, mix, residual, result, window, conv, *, lon_blocks, block_width
):
    core = lax.axis_index("chan")
    start = halo_start(block_start, core)
    cells = half.shape[0]
    window[:cells, :] = half[...]
    window[cells:, :] = half[: window.shape[0] - cells, :]
    rows = GROUP * block_width
    for group in range(lon_blocks // GROUP):
        halo_conv(
            group * GROUP, GROUP, start, lon_blocks, block_width,
            window.at[group * rows :, :], edge_filter, conv_local, conv,
        )
        here = slice(group * rows, (group + 1) * rows)
        result[here, :] = residual[here, :] + jnp.dot(conv[...], mix[...], preferred_element_type=jnp.float32)


def gelu(x):
    return 0.5 * x * (1.0 + lax.erf(x * 0.7071067811865476))


def tail_kernel(block_start, *refs, first, places, lon_blocks, block_width, pieces, ordered):
    halves, refs = refs[: len(pieces)], refs[len(pieces) + ordered :]
    (edge_filter, conv_local, partial, mix, up, up_other, down, down_other, keep, send, window, conv) = refs
    core = lax.axis_index("chan")
    start = halo_start(block_start, core)
    width = window.shape[1]
    at = 0
    for half, (low, high) in zip(halves, pieces):
        window[at : at + high - low, :] = half[low:high, :]
        at += high - low
    halo_conv(first, places, start, lon_blocks, block_width, window, edge_filter, conv_local, conv)
    mixed = jnp.dot(conv[...], mix[...], preferred_element_type=jnp.float32)
    state = partial[first * block_width : (first + places) * block_width, :] + mixed
    rounded = state.astype(jnp.bfloat16)
    total = state
    for inward, outward in ((up, down), (up_other, down_other)):
        hidden = gelu(jnp.dot(rounded, inward[...], preferred_element_type=jnp.float32)).astype(jnp.bfloat16)
        total += jnp.dot(hidden, outward[...], preferred_element_type=jnp.float32)
    total = total.astype(jnp.bfloat16)
    low, high = total[:, :width], total[:, width:]
    keep[...] = jnp.where(core == 0, low, high)
    send[...] = jnp.where(core == 0, high, low)


def stage_kernel(*refs):
    *refs, sems = refs
    count = len(refs) // 2
    wait_all(start_all([
        pltpu.make_async_copy(refs[index], refs[count + index], sems.at[index]) for index in range(count)
    ]))


def place_kernel(block_start, *refs, kept, received, lon_blocks, block_width):
    result, sems = refs[-2:]
    core = lax.axis_index("chan")
    jobs = []
    for index, (source, first) in enumerate(zip(refs, kept + received)):
        row = core if index < len(kept) else 1 - core
        places = source.shape[0] // block_width
        home = home_block(first, halo_start(block_start, row), lon_blocks)
        before_wrap = jnp.minimum(lon_blocks - home, places)
        for count in range(1, places + 1):
            size = count * block_width
            copies = [pltpu.make_async_copy(
                source.at[:size, :], result.at[row, block_rows(home, block_width, count), :], sems.at[index, 0]
            )]
            if count < places:
                copies.append(pltpu.make_async_copy(
                    source.at[size:, :], result.at[row, : source.shape[0] - size, :], sems.at[index, 1]
                ))
            jobs.append((before_wrap == count, copies))
    for started in (True, False):
        for chosen, copies in jobs:

            @pl.when(chosen)
            def _():
                if started:
                    start_all(copies)
                else:
                    wait_all(copies)


def limit(mebibytes):
    return pltpu.CompilerParams(vmem_limit_bytes=mebibytes * 1024 * 1024)


def cost(flops=1000):
    return pl.CostEstimate(flops=flops, bytes_accessed=1000, transcendentals=0)


def anywhere(count):
    return [pl.BlockSpec(memory_space=pl.ANY)] * count


def vmem(count):
    return [pl.BlockSpec(memory_space=pltpu.VMEM)] * count


def per_device(
    state_in, basis_blocks, block_start, block_count, mix_weight, up_weight, down_weight
):
    core = lax.axis_index("chan")
    bands = lax.axis_size("lat")
    local_rows, basis_count, block_width, taps, block_most = basis_blocks.shape[:5]
    cells, width = state_in.shape[1:]
    channels = mix_weight.shape[2]
    lon_blocks = cells // block_width
    depth = block_most * block_width
    filter_rows = basis_count * block_width
    swap = [(0, 1), (1, 0)]
    pairs = []
    for band in range(bands - 1):
        pairs += [(2 * band + 1, 2 * band + 2), (2 * band + 2, 2 * band + 1)]

    sizes = dict(block_width=block_width, lon_blocks=lon_blocks)
    smem = [pl.BlockSpec(memory_space=pltpu.SMEM)]
    cut = (FIRST + block_most - 1) * block_width
    edge, state_in = lax.optimization_barrier((state_in[core], state_in))
    halo_other = lax.ppermute(edge, ("lat", "chan"), pairs)
    other = lax.ppermute(state_in, "chan", swap)
    relay = other[core]
    halo_first = lax.ppermute(relay[:cut], ("lat", "chan"), pairs)
    halo_last = lax.ppermute(relay[cut:], ("lat", "chan"), pairs)
    basis_flat = basis_blocks.reshape(local_rows * filter_rows * taps * block_most, block_width)
    near_filter, edge_filter = pl.pallas_call(
        functools.partial(filter_kernel, block_most=block_most),
        out_shape=[
            jax.ShapeDtypeStruct((filter_rows, span * depth), jnp.bfloat16) for span in (taps - 1, 1)
        ],
        in_specs=smem + anywhere(1),
        out_specs=vmem(2),
        scratch_shapes=[
            pltpu.VMEM((basis_flat.shape[0] // local_rows, block_width), jnp.bfloat16),
            pltpu.VMEM((taps, filter_rows, depth), jnp.bfloat16),
            pltpu.SemaphoreType.DMA,
        ],
        compiler_params=limit(8),
        cost_estimate=cost(),
        name="spread_filters",
    )(block_count, basis_flat)
    mix_other = lax.ppermute(mix_weight, "chan", swap)
    up_other = lax.ppermute(up_weight, "chan", swap)
    down_other = lax.ppermute(down_weight, "chan", swap)

    conv_shape = jax.ShapeDtypeStruct((lon_blocks, filter_rows, width), jnp.float32)
    wide_window = pltpu.VMEM((cells + depth - block_width, channels), jnp.bfloat16)
    state_shape = jax.ShapeDtypeStruct((cells, channels), jnp.float32)
    conv_own, conv_other, residual = pl.pallas_call(
        functools.partial(local_kernel, block_most=block_most, **sizes),
        out_shape=(conv_shape, conv_shape, state_shape),
        in_specs=smem + vmem(3),
        out_specs=vmem(3),
        scratch_shapes=[wide_window, wide_window],
        compiler_params=limit(14),
        cost_estimate=cost(),
        name="local_taps",
    )(block_start, near_filter, state_in, other)

    weights = (
        mix_other.reshape(basis_count * width, channels), mix_weight.reshape(basis_count * width, channels),
        up_weight, up_other, down_weight, down_other,
    )
    mix_other, *weights = pl.pallas_call(
        stage_kernel,
        out_shape=[jax.ShapeDtypeStruct(array.shape, array.dtype) for array in weights],
        in_specs=anywhere(len(weights)),
        out_specs=vmem(len(weights)),
        scratch_shapes=[pltpu.SemaphoreType.DMA((len(weights),))],
        compiler_params=limit(8),
        cost_estimate=cost(),
        name="stage_weights",
    )(*weights)

    partial = pl.pallas_call(
        functools.partial(first_half_kernel, **sizes),
        out_shape=state_shape,
        in_specs=smem + vmem(5),
        out_specs=vmem(1)[0],
        scratch_shapes=[
            pltpu.VMEM((cells + depth - block_width, width), jnp.bfloat16),
            pltpu.VMEM((GROUP * block_width, basis_count * width), jnp.bfloat16),
        ],
        input_output_aliases={5: 0},
        compiler_params=limit(14),
        cost_estimate=cost(),
        name="edge_tap_first_half",
    )(block_start, halo_other, edge_filter, conv_other, mix_other, residual)

    overlap = (block_most - 1) * block_width
    plans = (
        (0, FIRST, [(0, cut)], (halo_first,)),
        (
            FIRST, lon_blocks - FIRST,
            [(cut - overlap, cut), (0, cells - cut), (0, overlap)], (halo_first, halo_last, halo_first),
        ),
    )
    kept, received, done = [], [], []
    for first, places, pieces, halves in plans:
        half = jax.ShapeDtypeStruct((places * block_width, width), jnp.bfloat16)
        keep, send = pl.pallas_call(
            functools.partial(
                tail_kernel, first=first, places=places, pieces=pieces, ordered=len(done), **sizes
            ),
            out_shape=(half, half),
            in_specs=smem + vmem(len(pieces)) + anywhere(len(done)) + vmem(8),
            out_specs=vmem(2),
            scratch_shapes=[
                pltpu.VMEM(((places + block_most - 1) * block_width, width), jnp.bfloat16),
                pltpu.VMEM((places * block_width, basis_count * width), jnp.bfloat16),
            ],
            compiler_params=limit(14),
            cost_estimate=cost(10**10 if done else 1000),
            name="edge_tap_and_feed",
        )(block_start, *halves, *done, edge_filter, conv_own, partial, *weights)
        if received:
            send, received[-1] = lax.optimization_barrier((send, received[-1]))
        kept.append(keep)
        done = [keep]
        received.append(lax.ppermute(send, "chan", swap))

    result = jax.ShapeDtypeStruct(state_in.shape, state_in.dtype)
    placed = pl.pallas_call(
        functools.partial(place_kernel, kept=[0, FIRST], received=[0], **sizes),
        out_shape=result,
        in_specs=smem + vmem(3),
        out_specs=anywhere(1)[0],
        scratch_shapes=[pltpu.SemaphoreType.DMA((3, 2))],
        cost_estimate=cost(),
        compiler_params=limit(4),
        name="place_rows",
    )(block_start, *kept, received[0])

    def place_last(starts, source, before, *refs):
        place_kernel(starts, source, *refs, kept=[], received=[FIRST], **sizes)

    return pl.pallas_call(
        place_last,
        out_shape=result,
        in_specs=smem + vmem(1) + anywhere(1),
        out_specs=anywhere(1)[0],
        scratch_shapes=[pltpu.SemaphoreType.DMA((1, 2))],
        input_output_aliases={2: 0},
        cost_estimate=cost(),
        compiler_params=limit(4),
        name="place_last_rows",
    )(block_start, received[1], placed)


def solution(mesh):
    placed = (
        P(("grp", "lat"), None, "chan"),
        P("lat", None, None, None, None, None),
        P("lat", None),
        P("lat", None),
        P(None, "chan", None),
        P(None, "chan"),
        P("chan", None),
    )
    return jax.shard_map(
        per_device,
        mesh=mesh,
        in_specs=placed,
        out_specs=P(("grp", "lat"), None, "chan"),
        check_vma=False,
    )
```

```python
import functools

import jax
import jax.numpy as jnp
from jax import lax
from jax.experimental import pallas as pl
from jax.experimental.pallas import tpu as pltpu
from jax.sharding import PartitionSpec as P

GROUP = 9
FIRST = 8
TILE = 16


def start_all(copies):
    for copy in copies:
        copy.start()
    return copies


def wait_all(copies):
    for copy in copies:
        copy.wait()


def halo_start(block_start, core):
    return block_start[core, 2 * core]


def block_rows(block, block_width, blocks=1):
    return pl.ds(pl.multiple_of(block * block_width, block_width), blocks * block_width)


def wrap(block, lon_blocks):
    return jnp.where(block >= lon_blocks, block - lon_blocks, block)


def home_block(place, start, lon_blocks):
    return jnp.where(place < start, place + lon_blocks - start, place - start)


def spread_filters(basis, counts, core, filters, block_most):
    rows_out, taps, width = filters.shape[1], filters.shape[0], basis.shape[1]
    pieces = taps * block_most
    size = TILE * pieces
    row = lax.broadcasted_iota(jnp.int32, (size, size), 0)
    column = lax.broadcasted_iota(jnp.int32, (size, size), 1)
    order = (column == lax.rem(row, TILE) * pieces + row // TILE).astype(jnp.float32).astype(jnp.bfloat16)
    for tile in range(rows_out // TILE):
        sorted_rows = jnp.dot(
            order, basis[tile * size : (tile + 1) * size, :], preferred_element_type=jnp.float32
        ).astype(jnp.bfloat16)
        for tap in range(taps):
            for block in range(block_most):
                at = (tap * block_most + block) * TILE
                piece = sorted_rows[at : at + TILE]
                filters[tap, tile * TILE : (tile + 1) * TILE, block * width : (block + 1) * width] = (
                    jnp.where(block < counts[core, tap], piece, jnp.zeros_like(piece))
                )


def filter_kernel(block_count, basis_from, near, edge, basis, filters, sem, *, block_most):
    core = lax.axis_index("chan")
    rows = basis.shape[0]
    depth = filters.shape[2]
    copy = pltpu.make_async_copy(
        basis_from.at[pl.ds(pl.multiple_of(core * rows, rows), rows), :], basis, sem
    )
    copy.start()
    copy.wait()
    spread_filters(basis, block_count, core, filters, block_most)
    near[:, :depth] = filters[1 - core]
    near[:, depth:] = filters[2 - core]
    edge[...] = filters[2 * core]


def local_kernel(
    block_start, near, own_from, other, conv_own, conv_other, residual, own, window0, window1, sem,
    *, lon_blocks, block_width, block_most,
):
    core = lax.axis_index("chan")
    cells, width = own.shape[1:]
    copy = pltpu.make_async_copy(own_from, own, sem)
    copy.start()
    copy.wait()
    for row, window in enumerate((window0, window1)):
        extra = window.shape[0] - cells
        for half, source in enumerate((own, other)):
            lanes = slice(half * width, (half + 1) * width)
            window[:cells, lanes] = source[row]
            window[cells:, lanes] = source[row, :extra]
    start = halo_start(block_start, core)
    for place in range(lon_blocks):
        source = block_rows(home_block(place, start, lon_blocks), block_width)
        target = slice(place * block_width, (place + 1) * block_width)
        mine = own[core, source, :].astype(jnp.float32)
        theirs = other[core, source, :].astype(jnp.float32)
        residual[target, :width] = jnp.where(core == 0, mine, theirs)
        residual[target, width:] = jnp.where(core == 0, theirs, mine)
    starts = (block_start[core, 1 - core], block_start[core, 2 - core])

    def group_step(group, carry):
        for slot in range(GROUP):
            place = group * GROUP + slot
            home = home_block(place, start, lon_blocks)
            parts = []
            for window, tap_start in zip((window0, window1), starts):
                source = wrap(home + tap_start, lon_blocks)
                parts.append(window[block_rows(source, block_width, block_most), :])
            result = jnp.dot(near[...], jnp.concatenate(parts, axis=0), preferred_element_type=jnp.float32)
            conv_own[place] = result[:, :width]
            conv_other[place] = result[:, width:]
        return carry

    lax.fori_loop(0, lon_blocks // GROUP, group_step, 0)


def halo_conv(first, places, block_width, window, edge_filter, conv_local, conv):
    depth = edge_filter.shape[1]
    width = window.shape[1]
    for slot in range(places):
        result = conv_local[first + slot] + jnp.dot(
            edge_filter[...], window[slot * block_width : slot * block_width + depth, :],
            preferred_element_type=jnp.float32,
        )
        rounded = result.astype(jnp.bfloat16)
        for basis in range(edge_filter.shape[0] // block_width):
            conv[
                slot * block_width : (slot + 1) * block_width, basis * width : (basis + 1) * width
            ] = rounded[basis * block_width : (basis + 1) * block_width]


def first_half_kernel(half, edge_filter, conv_local, mix, residual, result, window, conv, *, block_width):
    cells = half.shape[0]
    window[:cells, :] = half[...]
    window[cells:, :] = half[: window.shape[0] - cells, :]
    rows = GROUP * block_width
    for group in range(cells // rows):
        halo_conv(
            group * GROUP, GROUP, block_width, window.at[group * rows :, :], edge_filter, conv_local, conv
        )
        here = slice(group * rows, (group + 1) * rows)
        result[here, :] = residual[here, :] + jnp.dot(conv[...], mix[...], preferred_element_type=jnp.float32)


def gelu(x):
    return 0.5 * x * (1.0 + lax.erf(x * 0.7071067811865476))


def tail_kernel(*refs, first, places, block_width, pieces, ordered):
    halves, refs = refs[: len(pieces)], refs[len(pieces) + ordered :]
    (edge_filter, conv_local, partial, mix, up, up_other, down, down_other, keep, send, window, conv) = refs
    core = lax.axis_index("chan")
    width = window.shape[1]
    at = 0
    for half, (low, high) in zip(halves, pieces):
        window[at : at + high - low, :] = half[low:high, :]
        at += high - low
    halo_conv(first, places, block_width, window, edge_filter, conv_local, conv)
    mixed = jnp.dot(conv[...], mix[...], preferred_element_type=jnp.float32)
    state = partial[first * block_width : (first + places) * block_width, :] + mixed
    rounded = state.astype(jnp.bfloat16)
    total = state
    for inward, outward in ((up, down), (up_other, down_other)):
        hidden = gelu(jnp.dot(rounded, inward[...], preferred_element_type=jnp.float32)).astype(jnp.bfloat16)
        total += jnp.dot(hidden, outward[...], preferred_element_type=jnp.float32)
    total = total.astype(jnp.bfloat16)
    low, high = total[:, :width], total[:, width:]
    keep[...] = jnp.where(core == 0, low, high)
    send[...] = jnp.where(core == 0, high, low)


def stage_kernel(*refs):
    *refs, sems = refs
    count = len(refs) // 2
    wait_all(start_all([
        pltpu.make_async_copy(refs[index], refs[count + index], sems.at[index]) for index in range(count)
    ]))


def place_kernel(block_start, *refs, kept, received, lon_blocks, block_width):
    result, sems = refs[-2:]
    core = lax.axis_index("chan")
    jobs = []
    for index, (source, first) in enumerate(zip(refs, kept + received)):
        row = core if index < len(kept) else 1 - core
        home = home_block(first, halo_start(block_start, row), lon_blocks)
        jobs.append((source, row, home, source.shape[0] // block_width, sems.at[index]))

    def begin(job, count):
        source, row, home, places, sem = job
        size = count * block_width
        pltpu.make_async_copy(
            source.at[:size, :], result.at[row, block_rows(home, block_width, count), :], sem
        ).start()
        if count < places:
            pltpu.make_async_copy(
                source.at[size:, :], result.at[row, : source.shape[0] - size, :], sem
            ).start()

    def choose(job, low, high):
        if low == high:
            begin(job, low)
            return
        middle = (low + high) // 2
        early = lon_blocks - job[2] <= middle
        pl.when(early)(lambda: choose(job, low, middle))
        pl.when(jnp.logical_not(early))(lambda: choose(job, middle + 1, high))

    for job in jobs:
        choose(job, 1, job[3])
    for source, row, _, _, sem in jobs:
        pltpu.make_async_copy(source, result.at[row, : source.shape[0], :], sem).wait()


def relay_kernel(other, first, last):
    core = lax.axis_index("chan")
    cut = first.shape[0]
    first[...] = other[core, :cut, :]
    last[...] = other[core, cut:, :]


def edge_kernel(rows, result, sem):
    copy = pltpu.make_async_copy(rows.at[lax.axis_index("chan")], result, sem)
    copy.start()
    copy.wait()


def edge_row(rows):
    return pl.pallas_call(
        edge_kernel,
        out_shape=pltpu.VMEM(rows.shape[1:], rows.dtype),
        in_specs=anywhere(1),
        out_specs=vmem(1)[0],
        scratch_shapes=[pltpu.SemaphoreType.DMA],
        compiler_params=limit(4),
        cost_estimate=cost(),
        name="edge_row",
    )(in_hbm(rows))


def in_hbm(array):
    return pltpu.with_memory_space_constraint(array, pltpu.HBM)


def limit(mebibytes):
    return pltpu.CompilerParams(vmem_limit_bytes=mebibytes * 1024 * 1024)


def cost(flops=1000):
    return pl.CostEstimate(flops=flops, bytes_accessed=1000, transcendentals=0)


def anywhere(count):
    return [pl.BlockSpec(memory_space=pl.ANY)] * count


def vmem(count):
    return [pl.BlockSpec(memory_space=pltpu.VMEM)] * count


def per_device(
    state_in, basis_blocks, block_start, block_count, mix_weight, up_weight, down_weight
):
    core = lax.axis_index("chan")
    bands = lax.axis_size("lat")
    local_rows, basis_count, block_width, taps, block_most = basis_blocks.shape[:5]
    cells, width = state_in.shape[1:]
    channels = mix_weight.shape[2]
    lon_blocks = cells // block_width
    depth = block_most * block_width
    filter_rows = basis_count * block_width
    swap = [(0, 1), (1, 0)]
    pairs = []
    for band in range(bands - 1):
        pairs += [(2 * band + 1, 2 * band + 2), (2 * band + 2, 2 * band + 1)]

    sizes = dict(block_width=block_width, lon_blocks=lon_blocks)
    smem = [pl.BlockSpec(memory_space=pltpu.SMEM)]
    cut = (FIRST + block_most - 1) * block_width
    edge = edge_row(state_in)
    halo_other = lax.ppermute(edge, ("lat", "chan"), pairs)
    other = lax.ppermute(state_in, "chan", swap)
    relay = pl.pallas_call(
        relay_kernel,
        out_shape=[jax.ShapeDtypeStruct((rows, width), state_in.dtype) for rows in (cut, cells - cut)],
        in_specs=vmem(1),
        out_specs=vmem(2),
        compiler_params=limit(4),
        cost_estimate=cost(),
        name="relay_rows",
    )(other)
    halo_first, halo_last = [lax.ppermute(rows, ("lat", "chan"), pairs) for rows in relay]
    basis_flat = basis_blocks.reshape(local_rows * filter_rows * taps * block_most, block_width)
    near_filter, edge_filter = pl.pallas_call(
        functools.partial(filter_kernel, block_most=block_most),
        out_shape=[
            jax.ShapeDtypeStruct((filter_rows, span * depth), jnp.bfloat16) for span in (taps - 1, 1)
        ],
        in_specs=smem + anywhere(1),
        out_specs=vmem(2),
        scratch_shapes=[
            pltpu.VMEM((basis_flat.shape[0] // local_rows, block_width), jnp.bfloat16),
            pltpu.VMEM((taps, filter_rows, depth), jnp.bfloat16),
            pltpu.SemaphoreType.DMA,
        ],
        compiler_params=limit(8),
        cost_estimate=cost(),
        name="spread_filters",
    )(block_count, in_hbm(basis_flat))
    mix_other = lax.ppermute(mix_weight, "chan", swap)
    up_other = lax.ppermute(up_weight, "chan", swap)
    down_other = lax.ppermute(down_weight, "chan", swap)

    conv_shape = jax.ShapeDtypeStruct((lon_blocks, filter_rows, width), jnp.float32)
    wide_window = pltpu.VMEM((cells + depth - block_width, channels), jnp.bfloat16)
    state_shape = jax.ShapeDtypeStruct((cells, channels), jnp.float32)
    conv_own, conv_other, residual = pl.pallas_call(
        functools.partial(local_kernel, block_most=block_most, **sizes),
        out_shape=(conv_shape, conv_shape, state_shape),
        in_specs=smem + vmem(1) + anywhere(1) + vmem(1),
        out_specs=vmem(3),
        scratch_shapes=[
            pltpu.VMEM(state_in.shape, state_in.dtype), wide_window, wide_window, pltpu.SemaphoreType.DMA
        ],
        compiler_params=limit(14),
        cost_estimate=cost(),
        name="local_taps",
    )(block_start, near_filter, in_hbm(state_in), other)

    weights = (
        mix_other.reshape(basis_count * width, channels),
        in_hbm(mix_weight.reshape(basis_count * width, channels)),
        in_hbm(up_weight), up_other, in_hbm(down_weight), down_other,
    )
    mix_other, *weights = pl.pallas_call(
        stage_kernel,
        out_shape=[jax.ShapeDtypeStruct(array.shape, array.dtype) for array in weights],
        in_specs=anywhere(len(weights)),
        out_specs=vmem(len(weights)),
        scratch_shapes=[pltpu.SemaphoreType.DMA((len(weights),))],
        compiler_params=limit(8),
        cost_estimate=cost(),
        name="stage_weights",
    )(*weights)

    partial = pl.pallas_call(
        functools.partial(first_half_kernel, block_width=block_width),
        out_shape=state_shape,
        in_specs=vmem(5),
        out_specs=vmem(1)[0],
        scratch_shapes=[
            pltpu.VMEM((cells + depth - block_width, width), jnp.bfloat16),
            pltpu.VMEM((GROUP * block_width, basis_count * width), jnp.bfloat16),
        ],
        input_output_aliases={4: 0},
        compiler_params=limit(14),
        cost_estimate=cost(),
        name="edge_tap_first_half",
    )(halo_other, edge_filter, conv_other, mix_other, residual)

    overlap = (block_most - 1) * block_width
    plans = (
        (0, FIRST, [(0, cut)], (halo_first,)),
        (
            FIRST, lon_blocks - FIRST,
            [(cut - overlap, cut), (0, cells - cut), (0, overlap)], (halo_first, halo_last, halo_first),
        ),
    )
    kept, received, done = [], [], []
    for first, places, pieces, halves in plans:
        half = jax.ShapeDtypeStruct((places * block_width, width), jnp.bfloat16)
        keep, send = pl.pallas_call(
            functools.partial(
                tail_kernel, first=first, places=places, pieces=pieces, ordered=len(done), block_width=block_width
            ),
            out_shape=(half, half),
            in_specs=vmem(len(pieces)) + anywhere(len(done)) + vmem(8),
            out_specs=vmem(2),
            scratch_shapes=[
                pltpu.VMEM(((places + block_most - 1) * block_width, width), jnp.bfloat16),
                pltpu.VMEM((places * block_width, basis_count * width), jnp.bfloat16),
            ],
            compiler_params=limit(14),
            cost_estimate=cost(10**10 if done else 1000),
            name="edge_tap_and_feed",
        )(*halves, *done, edge_filter, conv_own, partial, *weights)
        if received:
            send, received[-1] = lax.optimization_barrier((send, received[-1]))
        kept.append(keep)
        done = [keep]
        received.append(lax.ppermute(send, "chan", swap))

    result = jax.ShapeDtypeStruct(state_in.shape, state_in.dtype)
    placed = pl.pallas_call(
        functools.partial(place_kernel, kept=[0, FIRST], received=[0], **sizes),
        out_shape=result,
        in_specs=smem + vmem(3),
        out_specs=anywhere(1)[0],
        scratch_shapes=[pltpu.SemaphoreType.DMA((3,))],
        cost_estimate=cost(),
        compiler_params=limit(4),
        name="place_rows",
    )(block_start, *kept, received[0])

    def place_last(starts, source, before, *refs):
        place_kernel(starts, source, *refs, kept=[], received=[FIRST], **sizes)

    return pl.pallas_call(
        place_last,
        out_shape=result,
        in_specs=smem + vmem(1) + anywhere(1),
        out_specs=anywhere(1)[0],
        scratch_shapes=[pltpu.SemaphoreType.DMA((1,))],
        input_output_aliases={2: 0},
        cost_estimate=cost(),
        compiler_params=limit(4),
        name="place_last_rows",
    )(block_start, received[1], placed)


def solution(mesh):
    placed = (
        P(("grp", "lat"), None, "chan"),
        P("lat", None, None, None, None, None),
        P("lat", None),
        P("lat", None),
        P(None, "chan", None),
        P(None, "chan"),
        P("chan", None),
    )
    return jax.shard_map(
        per_device,
        mesh=mesh,
        in_specs=placed,
        out_specs=P(("grp", "lat"), None, "chan"),
        check_vma=False,
    )
```

```python
import functools

import jax
import jax.numpy as jnp
from jax import lax
from jax.experimental import pallas as pl
from jax.experimental.pallas import tpu as pltpu
from jax.sharding import PartitionSpec as P

GROUP = 9
TILE = 16
FIRST_CUTS = (0, 11, 18)
LAST_CUTS = (0, 8, 13, 18)


def start_all(copies):
    for copy in copies:
        copy.start()
    return copies


def wait_all(copies):
    for copy in copies:
        copy.wait()


def halo_start(block_start, core):
    return block_start[core, 2 * core]


def block_rows(block, block_width, blocks=1):
    return pl.ds(pl.multiple_of(block * block_width, block_width), blocks * block_width)


def wrap(block, lon_blocks):
    return jnp.where(block >= lon_blocks, block - lon_blocks, block)


def home_block(place, start, lon_blocks):
    return jnp.where(place < start, place + lon_blocks - start, place - start)


def spread_filters(basis, counts, core, filters, block_most):
    rows_out, taps, width = filters.shape[1], filters.shape[0], basis.shape[1]
    pieces = taps * block_most
    size = TILE * pieces
    row = lax.broadcasted_iota(jnp.int32, (size, size), 0)
    column = lax.broadcasted_iota(jnp.int32, (size, size), 1)
    order = (column == lax.rem(row, TILE) * pieces + row // TILE).astype(jnp.float32).astype(jnp.bfloat16)
    for tile in range(rows_out // TILE):
        sorted_rows = jnp.dot(
            order, basis[tile * size : (tile + 1) * size, :], preferred_element_type=jnp.float32
        ).astype(jnp.bfloat16)
        for tap in range(taps):
            for block in range(block_most):
                at = (tap * block_most + block) * TILE
                piece = sorted_rows[at : at + TILE]
                filters[tap, tile * TILE : (tile + 1) * TILE, block * width : (block + 1) * width] = (
                    jnp.where(block < counts[core, tap], piece, jnp.zeros_like(piece))
                )


def stage_weights(core, sources, targets, sem, width):
    (mix, mix_other, up, up_other, down, down_other) = sources
    (mix_to, mix_other_to, up_to, down_to) = targets
    pairs = []
    for place, half in enumerate((core, 1 - core)):
        theirs = pl.ds(pl.multiple_of(half * width, width), width)
        ours = slice(place * width, (place + 1) * width)
        pairs += [(mix.at[:, theirs], mix_to.at[:, ours]), (mix_other.at[:, theirs], mix_other_to.at[:, ours])]
        for index, (rows, columns) in enumerate(((up, down), (up_other, down_other))):
            units = slice(index * rows.shape[1], (index + 1) * rows.shape[1])
            pairs += [
                (rows.at[theirs, :], up_to.at[ours, units]),
                (columns.at[:, theirs], down_to.at[units, ours]),
            ]
    return [pltpu.make_async_copy(source, target, sem.at[index]) for index, (source, target) in enumerate(pairs)]


def local_kernel(
    block_start, block_count, basis_from, own_from, other, *refs, lon_blocks, block_width, block_most
):
    sources, refs = refs[:6], refs[6:]
    conv_own, conv_other, residual, edge_filter, *targets = refs[:8]
    own, basis, filters, near, window0, window1, own_sem, basis_sem, weight_sems = refs[8:]
    core = lax.axis_index("chan")
    cells, width = own.shape[1:]
    depth = block_most * block_width
    rows = basis.shape[0]
    first_copies = start_all([
        pltpu.make_async_copy(
            basis_from.at[pl.ds(pl.multiple_of(core * rows, rows), rows), :], basis, basis_sem
        ),
        pltpu.make_async_copy(own_from, own, own_sem),
    ])
    weight_copies = start_all(stage_weights(core, sources, targets, weight_sems, width))
    start = halo_start(block_start, core)
    fills = ((0, other), (1, own))
    for which, (half, source) in enumerate(fills):
        lanes = slice((1 - half) * width, (2 - half) * width)
        if which == 1:
            wait_all(first_copies)
        for row, window in enumerate((window0, window1)):
            window[:cells, lanes] = source[row]
            window[cells:, lanes] = source[row, : window.shape[0] - cells]
        for place in range(lon_blocks):
            home = block_rows(home_block(place, start, lon_blocks), block_width)
            residual[place * block_width : (place + 1) * block_width, lanes] = (
                source[core, home, :].astype(jnp.float32)
            )
    spread_filters(basis, block_count, core, filters, block_most)
    near[:, :depth] = filters[1 - core]
    near[:, depth:] = filters[2 - core]
    edge_filter[...] = filters[2 * core]
    starts = (block_start[core, 1 - core], block_start[core, 2 - core])

    def group_step(group, carry):
        for slot in range(GROUP):
            place = group * GROUP + slot
            home = home_block(place, start, lon_blocks)
            parts = []
            for window, tap_start in zip((window0, window1), starts):
                source = wrap(home + tap_start, lon_blocks)
                parts.append(window[block_rows(source, block_width, block_most), :])
            result = jnp.dot(near[...], jnp.concatenate(parts, axis=0), preferred_element_type=jnp.float32)
            conv_own[place] = result[:, :width]
            conv_other[place] = result[:, width:]
        return carry

    lax.fori_loop(0, lon_blocks // GROUP, group_step, 0)
    wait_all(weight_copies)


def halo_mix(first, places, block_width, halves, spans, edge_filter, conv_local, mix, window, conv):
    at = 0
    for half, (low, high) in zip(halves, spans):
        window[at : at + high - low, :] = half[low:high, :]
        at += high - low
    depth = edge_filter.shape[1]
    width = window.shape[1]
    for slot in range(places):
        result = conv_local[first + slot] + jnp.dot(
            edge_filter[...], window[slot * block_width : slot * block_width + depth, :],
            preferred_element_type=jnp.float32,
        )
        rounded = result.astype(jnp.bfloat16)
        for basis in range(edge_filter.shape[0] // block_width):
            conv[
                slot * block_width : (slot + 1) * block_width, basis * width : (basis + 1) * width
            ] = rounded[basis * block_width : (basis + 1) * block_width]
    return jnp.dot(conv[...], mix[...], preferred_element_type=jnp.float32)


def first_half_kernel(*refs, plan, ordered, block_width):
    halves, refs = refs[: len(plan["spans"])], refs[len(plan["spans"]) + ordered :]
    edge_filter, conv_local, mix, residual, result, window, conv = refs
    first, places = plan["first"], plan["places"]
    mixed = halo_mix(
        first, places, block_width, halves, plan["spans"], edge_filter, conv_local, mix, window, conv
    )
    result[...] = residual[first * block_width : (first + places) * block_width, :] + mixed


def gelu(x):
    return 0.5 * x * (1.0 + lax.erf(x * 0.7071067811865476))


def tail_kernel(*refs, plan, ordered, block_width, state_spans):
    count = len(plan["spans"])
    halves, refs = refs[:count], refs[count + ordered :]
    partials, refs = refs[: len(state_spans)], refs[len(state_spans) :]
    edge_filter, conv_local, mix, up, down, keep, send, window, conv = refs
    mixed = halo_mix(
        plan["first"], plan["places"], block_width, halves, plan["spans"], edge_filter, conv_local, mix,
        window, conv,
    )
    before = [partial[low:high, :] for partial, (low, high) in zip(partials, state_spans)]
    state = mixed + (before[0] if len(before) == 1 else jnp.concatenate(before, axis=0))
    width = send.shape[1]
    hidden = gelu(
        jnp.dot(state.astype(jnp.bfloat16), up[...], preferred_element_type=jnp.float32)
    ).astype(jnp.bfloat16)
    total = state + jnp.dot(hidden, down[...], preferred_element_type=jnp.float32)
    total = total.astype(jnp.bfloat16)
    first = plan["first"] * block_width
    keep[first : first + total.shape[0], :] = total[:, :width]
    send[...] = total[:, width:]


def begin_place(source, result, row, home, sem, lon_blocks, block_width):
    places = source.shape[0] // block_width

    def begin(count):
        size = count * block_width
        pltpu.make_async_copy(
            source.at[:size, :], result.at[row, block_rows(home, block_width, count), :], sem
        ).start()
        if count < places:
            pltpu.make_async_copy(
                source.at[size:, :], result.at[row, : source.shape[0] - size, :], sem
            ).start()

    def choose(low, high):
        if low == high:
            begin(low)
            return
        middle = (low + high) // 2
        early = lon_blocks - home <= middle
        pl.when(early)(lambda: choose(low, middle))
        pl.when(jnp.logical_not(early))(lambda: choose(middle + 1, high))

    choose(1, places)
    return pltpu.make_async_copy(source, result.at[row, : source.shape[0], :], sem)


def scalar_start(block_start, row):
    shape = block_start.shape
    here = jnp.logical_and(
        lax.broadcasted_iota(jnp.int32, shape, 0) == row, lax.broadcasted_iota(jnp.int32, shape, 1) == 2 * row
    )
    return jnp.max(jnp.where(here, block_start[...].astype(jnp.float32), 0.0)).astype(jnp.int32)


def place_kernel(block_start, keep, *refs, firsts, lon_blocks, block_width):
    *received, result, sems = refs
    core = lax.axis_index("chan")
    waits = []
    for index, (source, first) in enumerate(zip((keep, *received), (0, *firsts))):
        row = 1 - core if index else core
        if index < 2:
            start = scalar_start(block_start, row)
        waits.append(begin_place(
            source, result, row, home_block(first, start, lon_blocks), sems.at[index], lon_blocks, block_width
        ))
    wait_all(waits)


def place_last_kernel(block_start, source, before, result, sem, *, first, lon_blocks, block_width):
    row = 1 - lax.axis_index("chan")
    home = home_block(first, scalar_start(block_start, row), lon_blocks)
    begin_place(source, result, row, home, sem, lon_blocks, block_width).wait()


def relay_kernel(other, *pieces):
    core = lax.axis_index("chan")
    at = 0
    for piece in pieces:
        piece[...] = other[core, at : at + piece.shape[0], :]
        at += piece.shape[0]


def edge_kernel(rows, *refs):
    *pieces, sems = refs
    core = lax.axis_index("chan")
    at = 0
    copies = []
    for index, piece in enumerate(pieces):
        copies.append(
            pltpu.make_async_copy(rows.at[core, at : at + piece.shape[0], :], piece, sems.at[index])
        )
        at += piece.shape[0]
    wait_all(start_all(copies))


def in_hbm(array):
    return pltpu.with_memory_space_constraint(array, pltpu.HBM)


def limit(mebibytes):
    return pltpu.CompilerParams(vmem_limit_bytes=mebibytes * 1024 * 1024)


def cost(flops=1000):
    return pl.CostEstimate(flops=flops, bytes_accessed=1000, transcendentals=0)


def anywhere(count):
    return [pl.BlockSpec(memory_space=pl.ANY)] * count


def vmem(count):
    return [pl.BlockSpec(memory_space=pltpu.VMEM)] * count


def plans_of(cuts, lon_blocks, block_width, block_most):
    reach = block_most - 1
    plans = []
    first = 0
    for index in range(1, len(cuts)):
        last = cuts[index] - reach if index < len(cuts) - 1 else lon_blocks
        need = []
        for block in range(first, last + reach):
            block %= lon_blocks
            piece = max(which for which in range(len(cuts) - 1) if cuts[which] <= block)
            low = (block - cuts[piece]) * block_width
            if need and need[-1][0] == piece and need[-1][2] == low:
                need[-1][2] = low + block_width
            else:
                need.append([piece, low, low + block_width])
        plans.append(dict(
            first=first, places=last - first,
            pieces=[piece for piece, _, _ in need], spans=[(low, high) for _, low, high in need],
        ))
        first = last
    return plans


def per_device(
    state_in, basis_blocks, block_start, block_count, mix_weight, up_weight, down_weight
):
    bands = lax.axis_size("lat")
    local_rows, basis_count, block_width, taps, block_most = basis_blocks.shape[:5]
    cells, width = state_in.shape[1:]
    channels = mix_weight.shape[2]
    units = 2 * up_weight.shape[1]
    lon_blocks = cells // block_width
    depth = block_most * block_width
    filter_rows = basis_count * block_width
    swap = [(0, 1), (1, 0)]
    pairs = []
    for band in range(bands - 1):
        pairs += [(2 * band + 1, 2 * band + 2), (2 * band + 2, 2 * band + 1)]

    sizes = dict(block_width=block_width, lon_blocks=lon_blocks)
    smem = [pl.BlockSpec(memory_space=pltpu.SMEM)]
    narrow = state_in.dtype

    def row_pieces(cuts):
        return [pltpu.VMEM(((high - low) * block_width, width), narrow) for low, high in zip(cuts, cuts[1:])]

    edge = pl.pallas_call(
        edge_kernel,
        out_shape=row_pieces(FIRST_CUTS),
        in_specs=anywhere(1),
        out_specs=vmem(len(FIRST_CUTS) - 1),
        scratch_shapes=[pltpu.SemaphoreType.DMA((len(FIRST_CUTS) - 1,))],
        compiler_params=limit(4),
        cost_estimate=cost(),
        name="edge_row",
    )(in_hbm(state_in))
    halo_other = [lax.ppermute(piece, ("lat", "chan"), pairs) for piece in edge]
    other = lax.ppermute(state_in, "chan", swap)
    relay = pl.pallas_call(
        relay_kernel,
        out_shape=row_pieces(LAST_CUTS),
        in_specs=vmem(1),
        out_specs=vmem(len(LAST_CUTS) - 1),
        compiler_params=limit(4),
        cost_estimate=cost(),
        name="relay_rows",
    )(other)
    halo_own = [lax.ppermute(piece, ("lat", "chan"), pairs) for piece in relay]
    mix_other = lax.ppermute(mix_weight, "chan", swap)
    up_other = lax.ppermute(up_weight, "chan", swap)
    down_other = lax.ppermute(down_weight, "chan", swap)

    basis_flat = basis_blocks.reshape(local_rows * filter_rows * taps * block_most, block_width)
    mixing = (basis_count * width, channels)
    weights = (
        in_hbm(mix_weight.reshape(mixing)), mix_other.reshape(mixing),
        in_hbm(up_weight), up_other, in_hbm(down_weight), down_other,
    )
    conv_shape = jax.ShapeDtypeStruct((lon_blocks, filter_rows, width), jnp.float32)
    wide_window = pltpu.VMEM((cells + depth - block_width, channels), narrow)
    staged = [mixing, mixing, (channels, units), (units, channels)]
    conv_own, conv_other, residual, edge_filter, mix_own, mix_other, up, down = pl.pallas_call(
        functools.partial(local_kernel, block_most=block_most, **sizes),
        out_shape=[
            conv_shape, conv_shape, jax.ShapeDtypeStruct((cells, channels), jnp.float32),
            jax.ShapeDtypeStruct((filter_rows, depth), narrow),
            *[jax.ShapeDtypeStruct(shape, narrow) for shape in staged],
        ],
        in_specs=smem * 2 + anywhere(2) + vmem(1) + anywhere(len(weights)),
        out_specs=vmem(4 + len(staged)),
        scratch_shapes=[
            pltpu.VMEM(state_in.shape, narrow),
            pltpu.VMEM((basis_flat.shape[0] // local_rows, block_width), narrow),
            pltpu.VMEM((taps, filter_rows, depth), narrow),
            pltpu.VMEM((filter_rows, 2 * depth), narrow),
            wide_window, wide_window,
            pltpu.SemaphoreType.DMA, pltpu.SemaphoreType.DMA, pltpu.SemaphoreType.DMA((12,)),
        ],
        compiler_params=limit(16),
        cost_estimate=cost(),
        name="local_taps",
    )(block_start, block_count, in_hbm(basis_flat), in_hbm(state_in), other, *weights)

    def halo_scratch(plan):
        return [
            pltpu.VMEM(((plan["places"] + block_most - 1) * block_width, width), narrow),
            pltpu.VMEM((plan["places"] * block_width, basis_count * width), narrow),
        ]

    partials = []
    first_plans = plans_of(FIRST_CUTS, lon_blocks, block_width, block_most)
    for plan in first_plans:
        done = partials[-1:]
        partials.append(pl.pallas_call(
            functools.partial(first_half_kernel, plan=plan, ordered=len(done), block_width=block_width),
            out_shape=jax.ShapeDtypeStruct((plan["places"] * block_width, channels), jnp.float32),
            in_specs=vmem(len(plan["pieces"])) + anywhere(len(done)) + vmem(4),
            out_specs=vmem(1)[0],
            scratch_shapes=halo_scratch(plan),
            compiler_params=limit(10),
            cost_estimate=cost(4 * 10**9 if done else 1000),
            name="edge_tap_first_half",
        )(*[halo_other[piece] for piece in plan["pieces"]], *done, edge_filter, conv_other, mix_other, residual))

    received, done, firsts = [], partials[-1:], []
    last_plans = plans_of(LAST_CUTS, lon_blocks, block_width, block_most)
    for plan in last_plans:
        low, high = plan["first"], plan["first"] + plan["places"]
        states, state_spans = [], []
        for partial, other_plan in zip(partials, first_plans):
            begin = max(low, other_plan["first"])
            end = min(high, other_plan["first"] + other_plan["places"])
            if begin < end:
                states.append(partial)
                state_spans.append((
                    (begin - other_plan["first"]) * block_width, (end - other_plan["first"]) * block_width
                ))
        rows = plan["places"] * block_width
        keep, send = pl.pallas_call(
            functools.partial(
                tail_kernel, plan=plan, ordered=len(done), block_width=block_width, state_spans=state_spans
            ),
            out_shape=[jax.ShapeDtypeStruct((size, width), narrow) for size in (cells, rows)],
            in_specs=vmem(len(plan["pieces"])) + anywhere(len(done)) + vmem(len(states) + 5),
            out_specs=vmem(2),
            scratch_shapes=halo_scratch(plan),
            input_output_aliases={len(plan["pieces"]): 0} if received else {},
            compiler_params=limit(14),
            cost_estimate=cost(1000 if low == 0 else 10**10),
            name="edge_tap_and_feed",
        )(
            *[halo_own[piece] for piece in plan["pieces"]], *done, *states,
            edge_filter, conv_own, mix_own, up, down,
        )
        if received:
            send, received[-1] = lax.optimization_barrier((send, received[-1]))
        firsts.append(low)
        done = [keep]
        received.append(lax.ppermute(send, "chan", swap))

    result = jax.ShapeDtypeStruct(state_in.shape, narrow)
    placed = pl.pallas_call(
        functools.partial(place_kernel, firsts=firsts[:-1], **sizes),
        out_shape=result,
        in_specs=vmem(len(firsts) + 1),
        out_specs=anywhere(1)[0],
        scratch_shapes=[pltpu.SemaphoreType.DMA((len(firsts),))],
        cost_estimate=cost(),
        compiler_params=limit(4),
        name="place_rows",
    )(block_start, keep, *received[:-1])

    return pl.pallas_call(
        functools.partial(place_last_kernel, first=firsts[-1], **sizes),
        out_shape=result,
        in_specs=vmem(2) + anywhere(1),
        out_specs=anywhere(1)[0],
        scratch_shapes=[pltpu.SemaphoreType.DMA],
        input_output_aliases={2: 0},
        cost_estimate=cost(),
        compiler_params=limit(4),
        name="place_last_rows",
    )(block_start, received[-1], placed)


def solution(mesh):
    placed = (
        P(("grp", "lat"), None, "chan"),
        P("lat", None, None, None, None, None),
        P("lat", None),
        P("lat", None),
        P(None, "chan", None),
        P(None, "chan"),
        P("chan", None),
    )
    return jax.shard_map(
        per_device,
        mesh=mesh,
        in_specs=placed,
        out_specs=P(("grp", "lat"), None, "chan"),
        check_vma=False,
    )
```

```python
import functools

import jax
import jax.numpy as jnp
from jax import lax
from jax.experimental import pallas as pl
from jax.experimental.pallas import tpu as pltpu
from jax.sharding import PartitionSpec as P

GROUP = 9
TILE = 16
FIRST_CUTS = (0, 18)
LAST_CUTS = (0, 8, 13, 18)


def start_all(copies):
    for copy in copies:
        copy.start()
    return copies


def wait_all(copies):
    for copy in copies:
        copy.wait()


def halo_start(block_start, core):
    return block_start[core, 2 * core]


def block_rows(block, block_width, blocks=1):
    return pl.ds(pl.multiple_of(block * block_width, block_width), blocks * block_width)


def wrap(block, lon_blocks):
    return jnp.where(block >= lon_blocks, block - lon_blocks, block)


def home_block(place, start, lon_blocks):
    return jnp.where(place < start, place + lon_blocks - start, place - start)


def spread_filters(basis, counts, core, filters, block_most):
    rows_out, taps, width = filters.shape[1], filters.shape[0], basis.shape[1]
    pieces = taps * block_most
    size = TILE * pieces
    row = lax.broadcasted_iota(jnp.int32, (size, size), 0)
    column = lax.broadcasted_iota(jnp.int32, (size, size), 1)
    order = (column == lax.rem(row, TILE) * pieces + row // TILE).astype(jnp.float32).astype(jnp.bfloat16)
    for tile in range(rows_out // TILE):
        sorted_rows = jnp.dot(
            order, basis[tile * size : (tile + 1) * size, :], preferred_element_type=jnp.float32
        ).astype(jnp.bfloat16)
        for tap in range(taps):
            for block in range(block_most):
                at = (tap * block_most + block) * TILE
                piece = sorted_rows[at : at + TILE]
                filters[tap, tile * TILE : (tile + 1) * TILE, block * width : (block + 1) * width] = (
                    jnp.where(block < counts[core, tap], piece, jnp.zeros_like(piece))
                )


def stage_weights(core, sources, targets, sem, width):
    (mix, mix_other, up, up_other, down, down_other) = sources
    (mix_to, mix_other_to, up_to, down_to) = targets
    pairs = []
    for place, half in enumerate((core, 1 - core)):
        theirs = pl.ds(pl.multiple_of(half * width, width), width)
        ours = slice(place * width, (place + 1) * width)
        pairs += [(mix.at[:, theirs], mix_to.at[:, ours]), (mix_other.at[:, theirs], mix_other_to.at[:, ours])]
        for index, (rows, columns) in enumerate(((up, down), (up_other, down_other))):
            units = slice(index * rows.shape[1], (index + 1) * rows.shape[1])
            pairs += [
                (rows.at[theirs, :], up_to.at[ours, units]),
                (columns.at[:, theirs], down_to.at[units, ours]),
            ]
    return [pltpu.make_async_copy(source, target, sem.at[index]) for index, (source, target) in enumerate(pairs)]


def local_kernel(
    block_start, block_count, basis_from, own_from, other, *refs, lon_blocks, block_width, block_most
):
    sources, refs = refs[:6], refs[6:]
    conv_own, conv_other, residual, edge_filter, *targets = refs[:8]
    own, basis, filters, near, window0, window1, own_sem, basis_sem, weight_sems = refs[8:]
    core = lax.axis_index("chan")
    cells, width = own.shape[1:]
    depth = block_most * block_width
    rows = basis.shape[0]
    first_copies = start_all([
        pltpu.make_async_copy(
            basis_from.at[pl.ds(pl.multiple_of(core * rows, rows), rows), :], basis, basis_sem
        ),
        pltpu.make_async_copy(own_from, own, own_sem),
    ])
    weight_copies = start_all(stage_weights(core, sources, targets, weight_sems, width))
    start = halo_start(block_start, core)
    fills = ((0, other), (1, own))
    for which, (half, source) in enumerate(fills):
        lanes = slice((1 - half) * width, (2 - half) * width)
        if which == 1:
            wait_all(first_copies)
        for row, window in enumerate((window0, window1)):
            window[:cells, lanes] = source[row]
            window[cells:, lanes] = source[row, : window.shape[0] - cells]
        for place in range(lon_blocks):
            home = block_rows(home_block(place, start, lon_blocks), block_width)
            residual[place * block_width : (place + 1) * block_width, lanes] = (
                source[core, home, :].astype(jnp.float32)
            )
    spread_filters(basis, block_count, core, filters, block_most)
    near[:, :depth] = filters[1 - core]
    near[:, depth:] = filters[2 - core]
    edge_filter[...] = filters[2 * core]
    starts = (block_start[core, 1 - core], block_start[core, 2 - core])

    def group_step(group, carry):
        for slot in range(GROUP):
            place = group * GROUP + slot
            home = home_block(place, start, lon_blocks)
            parts = []
            for window, tap_start in zip((window0, window1), starts):
                source = wrap(home + tap_start, lon_blocks)
                parts.append(window[block_rows(source, block_width, block_most), :])
            result = jnp.dot(near[...], jnp.concatenate(parts, axis=0), preferred_element_type=jnp.float32)
            conv_own[place] = result[:, :width]
            conv_other[place] = result[:, width:]
        return carry

    lax.fori_loop(0, lon_blocks // GROUP, group_step, 0)
    wait_all(weight_copies)


def halo_mix(first, places, block_width, halves, spans, edge_filter, conv_local, mix, window, conv):
    at = 0
    for half, (low, high) in zip(halves, spans):
        window[at : at + high - low, :] = half[low:high, :]
        at += high - low
    depth = edge_filter.shape[1]
    width = window.shape[1]
    for slot in range(places):
        result = conv_local[first + slot] + jnp.dot(
            edge_filter[...], window[slot * block_width : slot * block_width + depth, :],
            preferred_element_type=jnp.float32,
        )
        rounded = result.astype(jnp.bfloat16)
        for basis in range(edge_filter.shape[0] // block_width):
            conv[
                slot * block_width : (slot + 1) * block_width, basis * width : (basis + 1) * width
            ] = rounded[basis * block_width : (basis + 1) * block_width]
    return jnp.dot(conv[...], mix[...], preferred_element_type=jnp.float32)


def first_half_kernel(*refs, plan, ordered, block_width):
    halves, refs = refs[: len(plan["spans"])], refs[len(plan["spans"]) + ordered :]
    edge_filter, conv_local, mix, residual, result, window, conv = refs
    first, places = plan["first"], plan["places"]
    mixed = halo_mix(
        first, places, block_width, halves, plan["spans"], edge_filter, conv_local, mix, window, conv
    )
    result[...] = residual[first * block_width : (first + places) * block_width, :] + mixed


def gelu(x):
    return 0.5 * x * (1.0 + lax.erf(x * 0.7071067811865476))


def tail_kernel(*refs, plan, ordered, block_width, state_spans):
    count = plan["all"]
    halves, refs = [refs[piece] for piece in plan["pieces"]], refs[count + ordered :]
    partials, refs = refs[: len(state_spans)], refs[len(state_spans) :]
    edge_filter, conv_local, mix, up, down, keep, send, window, conv = refs
    mixed = halo_mix(
        plan["first"], plan["places"], block_width, halves, plan["spans"], edge_filter, conv_local, mix,
        window, conv,
    )
    before = [partial[low:high, :] for partial, (low, high) in zip(partials, state_spans)]
    state = mixed + (before[0] if len(before) == 1 else jnp.concatenate(before, axis=0))
    width = send.shape[1]
    hidden = gelu(
        jnp.dot(state.astype(jnp.bfloat16), up[...], preferred_element_type=jnp.float32)
    ).astype(jnp.bfloat16)
    total = state + jnp.dot(hidden, down[...], preferred_element_type=jnp.float32)
    total = total.astype(jnp.bfloat16)
    first = plan["first"] * block_width
    keep[first : first + total.shape[0], :] = total[:, :width]
    first -= plan["sent_from"] * block_width
    send[first : first + total.shape[0], :] = total[:, width:]


def begin_place(source, result, row, home, sem, lon_blocks, block_width):
    places = source.shape[0] // block_width

    def begin(count):
        size = count * block_width
        pltpu.make_async_copy(
            source.at[:size, :], result.at[row, block_rows(home, block_width, count), :], sem
        ).start()
        if count < places:
            pltpu.make_async_copy(
                source.at[size:, :], result.at[row, : source.shape[0] - size, :], sem
            ).start()

    def choose(low, high):
        if low == high:
            begin(low)
            return
        middle = (low + high) // 2
        early = lon_blocks - home <= middle
        pl.when(early)(lambda: choose(low, middle))
        pl.when(jnp.logical_not(early))(lambda: choose(middle + 1, high))

    choose(1, places)
    return pltpu.make_async_copy(source, result.at[row, : source.shape[0], :], sem)


def scalar_start(block_start, row):
    shape = block_start.shape
    here = jnp.logical_and(
        lax.broadcasted_iota(jnp.int32, shape, 0) == row, lax.broadcasted_iota(jnp.int32, shape, 1) == 2 * row
    )
    return jnp.max(jnp.where(here, block_start[...].astype(jnp.float32), 0.0)).astype(jnp.int32)


def place_kernel(block_start, keep, *refs, firsts, lon_blocks, block_width):
    *received, result, sems = refs
    core = lax.axis_index("chan")
    waits = []
    for index, (source, first) in enumerate(zip((keep, *received), (0, *firsts))):
        row = 1 - core if index else core
        if index < 2:
            start = scalar_start(block_start, row)
        waits.append(begin_place(
            source, result, row, home_block(first, start, lon_blocks), sems.at[index], lon_blocks, block_width
        ))
    wait_all(waits)


def place_last_kernel(block_start, source, before, result, sem, *, first, lon_blocks, block_width):
    row = 1 - lax.axis_index("chan")
    home = home_block(first, scalar_start(block_start, row), lon_blocks)
    begin_place(source, result, row, home, sem, lon_blocks, block_width).wait()


def relay_kernel(other, ordered, *pieces):
    core = lax.axis_index("chan")
    at = 0
    for piece in pieces:
        piece[...] = other[core, at : at + piece.shape[0], :]
        at += piece.shape[0]


def edge_kernel(rows, *refs):
    *pieces, sems = refs
    core = lax.axis_index("chan")
    at = 0
    copies = []
    for index, piece in enumerate(pieces):
        copies.append(
            pltpu.make_async_copy(rows.at[core, at : at + piece.shape[0], :], piece, sems.at[index])
        )
        at += piece.shape[0]
    wait_all(start_all(copies))


def in_hbm(array):
    return pltpu.with_memory_space_constraint(array, pltpu.HBM)


def limit(mebibytes):
    return pltpu.CompilerParams(vmem_limit_bytes=mebibytes * 1024 * 1024)


def cost(flops=1000):
    return pl.CostEstimate(flops=flops, bytes_accessed=1000, transcendentals=0)


def anywhere(count):
    return [pl.BlockSpec(memory_space=pl.ANY)] * count


def vmem(count):
    return [pl.BlockSpec(memory_space=pltpu.VMEM)] * count


def plans_of(cuts, lon_blocks, block_width, block_most):
    reach = block_most - 1
    plans = []
    first = 0
    for index in range(1, len(cuts)):
        last = cuts[index] - reach if index < len(cuts) - 1 else lon_blocks
        need = []
        for block in range(first, last + reach):
            block %= lon_blocks
            piece = max(which for which in range(len(cuts) - 1) if cuts[which] <= block)
            low = (block - cuts[piece]) * block_width
            if need and need[-1][0] == piece and need[-1][2] == low:
                need[-1][2] = low + block_width
            else:
                need.append([piece, low, low + block_width])
        plans.append(dict(
            first=first, places=last - first,
            pieces=[piece for piece, _, _ in need], spans=[(low, high) for _, low, high in need],
        ))
        first = last
    return plans


def per_device(
    state_in, basis_blocks, block_start, block_count, mix_weight, up_weight, down_weight
):
    bands = lax.axis_size("lat")
    local_rows, basis_count, block_width, taps, block_most = basis_blocks.shape[:5]
    cells, width = state_in.shape[1:]
    channels = mix_weight.shape[2]
    units = 2 * up_weight.shape[1]
    lon_blocks = cells // block_width
    depth = block_most * block_width
    filter_rows = basis_count * block_width
    swap = [(0, 1), (1, 0)]
    pairs = []
    for band in range(bands - 1):
        pairs += [(2 * band + 1, 2 * band + 2), (2 * band + 2, 2 * band + 1)]

    sizes = dict(block_width=block_width, lon_blocks=lon_blocks)
    smem = [pl.BlockSpec(memory_space=pltpu.SMEM)]
    narrow = state_in.dtype

    def row_pieces(cuts):
        return [pltpu.VMEM(((high - low) * block_width, width), narrow) for low, high in zip(cuts, cuts[1:])]

    edge = pl.pallas_call(
        edge_kernel,
        out_shape=row_pieces(FIRST_CUTS),
        in_specs=anywhere(1),
        out_specs=vmem(len(FIRST_CUTS) - 1),
        scratch_shapes=[pltpu.SemaphoreType.DMA((len(FIRST_CUTS) - 1,))],
        compiler_params=limit(4),
        cost_estimate=cost(),
        name="edge_row",
    )(in_hbm(state_in))
    halo_other = [lax.ppermute(piece, ("lat", "chan"), pairs) for piece in edge]
    other = lax.ppermute(state_in, "chan", swap)
    mix_other = lax.ppermute(mix_weight, "chan", swap)
    up_other = lax.ppermute(up_weight, "chan", swap)
    down_other = lax.ppermute(down_weight, "chan", swap)

    basis_flat = basis_blocks.reshape(local_rows * filter_rows * taps * block_most, block_width)
    mixing = (basis_count * width, channels)
    weights = (
        in_hbm(mix_weight.reshape(mixing)), mix_other.reshape(mixing),
        in_hbm(up_weight), up_other, in_hbm(down_weight), down_other,
    )
    conv_shape = jax.ShapeDtypeStruct((lon_blocks, filter_rows, width), jnp.float32)
    wide_window = pltpu.VMEM((cells + depth - block_width, channels), narrow)
    staged = [mixing, mixing, (channels, units), (units, channels)]
    conv_own, conv_other, residual, edge_filter, mix_own, mix_other, up, down = pl.pallas_call(
        functools.partial(local_kernel, block_most=block_most, **sizes),
        out_shape=[
            conv_shape, conv_shape, jax.ShapeDtypeStruct((cells, channels), jnp.float32),
            jax.ShapeDtypeStruct((filter_rows, depth), narrow),
            *[jax.ShapeDtypeStruct(shape, narrow) for shape in staged],
        ],
        in_specs=smem * 2 + anywhere(2) + vmem(1) + anywhere(len(weights)),
        out_specs=vmem(4 + len(staged)),
        scratch_shapes=[
            pltpu.VMEM(state_in.shape, narrow),
            pltpu.VMEM((basis_flat.shape[0] // local_rows, block_width), narrow),
            pltpu.VMEM((taps, filter_rows, depth), narrow),
            pltpu.VMEM((filter_rows, 2 * depth), narrow),
            wide_window, wide_window,
            pltpu.SemaphoreType.DMA, pltpu.SemaphoreType.DMA, pltpu.SemaphoreType.DMA((12,)),
        ],
        compiler_params=limit(16),
        cost_estimate=cost(),
        name="local_taps",
    )(block_start, block_count, in_hbm(basis_flat), in_hbm(state_in), other, *weights)

    relay = pl.pallas_call(
        relay_kernel,
        out_shape=row_pieces(LAST_CUTS),
        in_specs=vmem(1) + anywhere(1),
        out_specs=vmem(len(LAST_CUTS) - 1),
        compiler_params=limit(4),
        cost_estimate=cost(),
        name="relay_rows",
    )(other, edge_filter)
    halo_own = [lax.ppermute(piece, ("lat", "chan"), pairs) for piece in relay]

    def halo_scratch(plan):
        return [
            pltpu.VMEM(((plan["places"] + block_most - 1) * block_width, width), narrow),
            pltpu.VMEM((plan["places"] * block_width, basis_count * width), narrow),
        ]

    partials = []
    first_plans = plans_of(FIRST_CUTS, lon_blocks, block_width, block_most)
    for plan in first_plans:
        done = partials[-1:]
        partials.append(pl.pallas_call(
            functools.partial(first_half_kernel, plan=plan, ordered=len(done), block_width=block_width),
            out_shape=jax.ShapeDtypeStruct((plan["places"] * block_width, channels), jnp.float32),
            in_specs=vmem(len(plan["pieces"])) + anywhere(len(done)) + vmem(4),
            out_specs=vmem(1)[0],
            scratch_shapes=halo_scratch(plan),
            compiler_params=limit(10),
            cost_estimate=cost(6 * 10**10),
            name="edge_tap_first_half",
        )(*[halo_other[piece] for piece in plan["pieces"]], *done, edge_filter, conv_other, mix_other, residual))

    sends, done = {}, partials[-1:]
    last_plans = plans_of(LAST_CUTS, lon_blocks, block_width, block_most)
    firsts = (0, last_plans[-1]["first"])
    for plan in last_plans:
        low, high = plan["first"], plan["first"] + plan["places"]
        states, state_spans = [], []
        for partial, other_plan in zip(partials, first_plans):
            begin = max(low, other_plan["first"])
            end = min(high, other_plan["first"] + other_plan["places"])
            if begin < end:
                states.append(partial)
                state_spans.append((
                    (begin - other_plan["first"]) * block_width, (end - other_plan["first"]) * block_width
                ))
        plan["sent_from"] = max(place for place in firsts if place <= low)
        sent = (firsts[1] if plan["sent_from"] == 0 else lon_blocks) - plan["sent_from"]
        plan["all"] = max(plan["pieces"]) + 1
        aliases = {plan["all"] + index: index for index in range(len(done))} if low else {}
        used = [vmem(1) if piece in plan["pieces"] else anywhere(1) for piece in range(plan["all"])]
        keep, send = pl.pallas_call(
            functools.partial(
                tail_kernel, plan=plan, ordered=len(done), block_width=block_width, state_spans=state_spans
            ),
            out_shape=[jax.ShapeDtypeStruct((size, width), narrow) for size in (cells, sent * block_width)],
            in_specs=sum(used, []) + anywhere(len(done)) + vmem(len(states) + 5),
            out_specs=vmem(2),
            scratch_shapes=halo_scratch(plan),
            input_output_aliases=aliases,
            compiler_params=limit(14),
            cost_estimate=cost(10**10 if high == lon_blocks else 1000),
            name="edge_tap_and_feed",
        )(
            *halo_own[: plan["all"]], *done, *states,
            edge_filter, conv_own, mix_own, up, down,
        )
        sends[plan["sent_from"]] = send
        done = [keep] if high == firsts[1] else [keep, send]

    early = lax.ppermute(sends[0], "chan", swap)
    late, early = lax.optimization_barrier((sends[firsts[1]], early))
    late = lax.ppermute(late, "chan", swap)
    result = jax.ShapeDtypeStruct(state_in.shape, narrow)
    placed = pl.pallas_call(
        functools.partial(place_kernel, firsts=firsts[:-1], **sizes),
        out_shape=result,
        in_specs=vmem(len(firsts) + 1),
        out_specs=anywhere(1)[0],
        scratch_shapes=[pltpu.SemaphoreType.DMA((len(firsts),))],
        cost_estimate=cost(),
        compiler_params=limit(4),
        name="place_rows",
    )(block_start, keep, early)

    return pl.pallas_call(
        functools.partial(place_last_kernel, first=firsts[-1], **sizes),
        out_shape=result,
        in_specs=vmem(2) + anywhere(1),
        out_specs=anywhere(1)[0],
        scratch_shapes=[pltpu.SemaphoreType.DMA],
        input_output_aliases={2: 0},
        cost_estimate=cost(),
        compiler_params=limit(4),
        name="place_last_rows",
    )(block_start, late, placed)


def solution(mesh):
    placed = (
        P(("grp", "lat"), None, "chan"),
        P("lat", None, None, None, None, None),
        P("lat", None),
        P("lat", None),
        P(None, "chan", None),
        P(None, "chan"),
        P("chan", None),
    )
    return jax.shard_map(
        per_device,
        mesh=mesh,
        in_specs=placed,
        out_specs=P(("grp", "lat"), None, "chan"),
        check_vma=False,
    )
```

```python
import functools

import jax
import jax.numpy as jnp
from jax import lax
from jax.experimental import pallas as pl
from jax.experimental.pallas import tpu as pltpu
from jax.sharding import PartitionSpec as P

GROUP = 9
TILE = 16
FIRST_CUTS = (0, 18)
LAST_CUTS = (0, 8, 13, 18)


def start_all(copies):
    for copy in copies:
        copy.start()
    return copies


def wait_all(copies):
    for copy in copies:
        copy.wait()


def halo_start(block_start, core):
    return block_start[core, 2 * core]


def block_rows(block, block_width, blocks=1):
    return pl.ds(pl.multiple_of(block * block_width, block_width), blocks * block_width)


def wrap(block, lon_blocks):
    return jnp.where(block >= lon_blocks, block - lon_blocks, block)


def home_block(place, start, lon_blocks):
    return jnp.where(place < start, place + lon_blocks - start, place - start)


def spread_filters(basis, counts, core, filters, block_most):
    rows_out, taps, width = filters.shape[1], filters.shape[0], basis.shape[1]
    pieces = taps * block_most
    size = TILE * pieces
    row = lax.broadcasted_iota(jnp.int32, (size, size), 0)
    column = lax.broadcasted_iota(jnp.int32, (size, size), 1)
    order = (column == lax.rem(row, TILE) * pieces + row // TILE).astype(jnp.float32).astype(jnp.bfloat16)
    for tile in range(rows_out // TILE):
        sorted_rows = jnp.dot(
            order, basis[tile * size : (tile + 1) * size, :], preferred_element_type=jnp.float32
        ).astype(jnp.bfloat16)
        for tap in range(taps):
            for block in range(block_most):
                at = (tap * block_most + block) * TILE
                piece = sorted_rows[at : at + TILE]
                filters[tap, tile * TILE : (tile + 1) * TILE, block * width : (block + 1) * width] = (
                    jnp.where(block < counts[core, tap], piece, jnp.zeros_like(piece))
                )


def stage_weights(core, sources, targets, sem, width):
    (mix, mix_other, up, up_other, down, down_other) = sources
    (mix_to, mix_other_to, up_to, down_to) = targets
    pairs = []
    for place, half in enumerate((core, 1 - core)):
        theirs = pl.ds(pl.multiple_of(half * width, width), width)
        ours = slice(place * width, (place + 1) * width)
        pairs += [(mix.at[:, theirs], mix_to.at[:, ours]), (mix_other.at[:, theirs], mix_other_to.at[:, ours])]
        for index, (rows, columns) in enumerate(((up, down), (up_other, down_other))):
            units = slice(index * rows.shape[1], (index + 1) * rows.shape[1])
            pairs += [
                (rows.at[theirs, :], up_to.at[ours, units]),
                (columns.at[:, theirs], down_to.at[units, ours]),
            ]
    return [pltpu.make_async_copy(source, target, sem.at[index]) for index, (source, target) in enumerate(pairs)]


def local_kernel(
    block_start, block_count, basis_from, own_from, other, *refs, lon_blocks, block_width, block_most
):
    sources, refs = refs[:6], refs[6:]
    conv_own, conv_other, residual, edge_filter, *targets = refs[:8]
    own, basis, filters, near, window0, window1, own_sem, basis_sem, weight_sems = refs[8:]
    core = lax.axis_index("chan")
    cells, width = own.shape[1:]
    depth = block_most * block_width
    rows = basis.shape[0]
    first_copies = start_all([
        pltpu.make_async_copy(
            basis_from.at[pl.ds(pl.multiple_of(core * rows, rows), rows), :], basis, basis_sem
        ),
        pltpu.make_async_copy(own_from, own, own_sem),
    ])
    weight_copies = start_all(stage_weights(core, sources, targets, weight_sems, width))
    start = halo_start(block_start, core)
    fills = ((0, other), (1, own))
    for which, (half, source) in enumerate(fills):
        lanes = slice((1 - half) * width, (2 - half) * width)
        if which == 1:
            wait_all(first_copies)
        for row, window in enumerate((window0, window1)):
            window[:cells, lanes] = source[row]
            window[cells:, lanes] = source[row, : window.shape[0] - cells]
        for place in range(lon_blocks):
            home = block_rows(home_block(place, start, lon_blocks), block_width)
            residual[place * block_width : (place + 1) * block_width, lanes] = (
                source[core, home, :].astype(jnp.float32)
            )
    spread_filters(basis, block_count, core, filters, block_most)
    near[:, :depth] = filters[1 - core]
    near[:, depth:] = filters[2 - core]
    edge_filter[...] = filters[2 * core]
    starts = (block_start[core, 1 - core], block_start[core, 2 - core])

    def group_step(group, carry):
        for slot in range(GROUP):
            place = group * GROUP + slot
            home = home_block(place, start, lon_blocks)
            parts = []
            for window, tap_start in zip((window0, window1), starts):
                source = wrap(home + tap_start, lon_blocks)
                parts.append(window[block_rows(source, block_width, block_most), :])
            result = jnp.dot(near[...], jnp.concatenate(parts, axis=0), preferred_element_type=jnp.float32)
            conv_own[place] = result[:, :width]
            conv_other[place] = result[:, width:]
        return carry

    lax.fori_loop(0, lon_blocks // GROUP, group_step, 0)
    wait_all(weight_copies)


def by_count(rows, filters, block_width, body):
    depth = filters.shape[1]
    row = rows // lax.axis_size("lat") * lax.axis_index("lat") + lax.axis_index("chan")
    few = 3 * (rows - row) * (rows - row) < 2 * rows * rows
    short = min(depth, -(-(depth - block_width) // 128) * 128)
    pl.when(few)(lambda: body(short))
    pl.when(jnp.logical_not(few))(lambda: body(depth))


def halo_mix(depth, first, places, block_width, halves, spans, edge_filter, conv_local, mix, window, conv):
    at = 0
    for half, (low, high) in zip(halves, spans):
        window[at : at + high - low, :] = half[low:high, :]
        at += high - low
    width = window.shape[1]
    for slot in range(places):
        result = conv_local[first + slot] + jnp.dot(
            edge_filter[:, :depth], window[slot * block_width : slot * block_width + depth, :],
            preferred_element_type=jnp.float32,
        )
        rounded = result.astype(jnp.bfloat16)
        for basis in range(edge_filter.shape[0] // block_width):
            conv[
                slot * block_width : (slot + 1) * block_width, basis * width : (basis + 1) * width
            ] = rounded[basis * block_width : (basis + 1) * block_width]
    return jnp.dot(conv[...], mix[...], preferred_element_type=jnp.float32)


def first_half_kernel(*refs, plan, ordered, block_width, rows):
    halves, refs = refs[: len(plan["spans"])], refs[len(plan["spans"]) + ordered :]
    edge_filter, conv_local, mix, residual, result, window, conv = refs
    first, places = plan["first"], plan["places"]

    def body(depth):
        mixed = halo_mix(
            depth, first, places, block_width, halves, plan["spans"], edge_filter, conv_local, mix, window, conv
        )
        result[...] = residual[first * block_width : (first + places) * block_width, :] + mixed

    by_count(rows, edge_filter, block_width, body)


def gelu(x):
    return 0.5 * x * (1.0 + lax.erf(x * 0.7071067811865476))


def tail_kernel(*refs, plan, ordered, block_width, state_spans, rows):
    count = plan["all"]
    halves, refs = [refs[piece] for piece in plan["pieces"]], refs[count + ordered :]
    partials, refs = refs[: len(state_spans)], refs[len(state_spans) :]
    edge_filter, conv_local, mix, up, down, keep, send, window, conv = refs

    def body(depth):
        mixed = halo_mix(
            depth, plan["first"], plan["places"], block_width, halves, plan["spans"], edge_filter, conv_local, mix,
            window, conv,
        )
        before = [partial[low:high, :] for partial, (low, high) in zip(partials, state_spans)]
        state = mixed + (before[0] if len(before) == 1 else jnp.concatenate(before, axis=0))
        width = send.shape[1]
        hidden = gelu(
            jnp.dot(state.astype(jnp.bfloat16), up[...], preferred_element_type=jnp.float32)
        ).astype(jnp.bfloat16)
        total = state + jnp.dot(hidden, down[...], preferred_element_type=jnp.float32)
        total = total.astype(jnp.bfloat16)
        first = plan["first"] * block_width
        keep[first : first + total.shape[0], :] = total[:, :width]
        first -= plan["sent_from"] * block_width
        send[first : first + total.shape[0], :] = total[:, width:]

    by_count(rows, edge_filter, block_width, body)


def begin_place(source, result, row, home, sem, lon_blocks, block_width):
    places = source.shape[0] // block_width

    def begin(count):
        size = count * block_width
        pltpu.make_async_copy(
            source.at[:size, :], result.at[row, block_rows(home, block_width, count), :], sem
        ).start()
        if count < places:
            pltpu.make_async_copy(
                source.at[size:, :], result.at[row, : source.shape[0] - size, :], sem
            ).start()

    def choose(low, high):
        if low == high:
            begin(low)
            return
        middle = (low + high) // 2
        early = lon_blocks - home <= middle
        pl.when(early)(lambda: choose(low, middle))
        pl.when(jnp.logical_not(early))(lambda: choose(middle + 1, high))

    choose(1, places)
    return pltpu.make_async_copy(source, result.at[row, : source.shape[0], :], sem)


def scalar_start(block_start, row):
    shape = block_start.shape
    here = jnp.logical_and(
        lax.broadcasted_iota(jnp.int32, shape, 0) == row, lax.broadcasted_iota(jnp.int32, shape, 1) == 2 * row
    )
    return jnp.max(jnp.where(here, block_start[...].astype(jnp.float32), 0.0)).astype(jnp.int32)


def place_kernel(block_start, keep, *refs, firsts, lon_blocks, block_width):
    *received, result, sems = refs
    core = lax.axis_index("chan")
    waits = []
    for index, (source, first) in enumerate(zip((keep, *received), (0, *firsts))):
        row = 1 - core if index else core
        if index < 2:
            start = scalar_start(block_start, row)
        waits.append(begin_place(
            source, result, row, home_block(first, start, lon_blocks), sems.at[index], lon_blocks, block_width
        ))
    wait_all(waits)


def place_last_kernel(block_start, source, before, result, sem, *, first, lon_blocks, block_width):
    row = 1 - lax.axis_index("chan")
    home = home_block(first, scalar_start(block_start, row), lon_blocks)
    begin_place(source, result, row, home, sem, lon_blocks, block_width).wait()


def relay_kernel(other, ordered, *pieces):
    core = lax.axis_index("chan")
    at = 0
    for piece in pieces:
        piece[...] = other[core, at : at + piece.shape[0], :]
        at += piece.shape[0]


def edge_kernel(rows, *refs):
    *pieces, sems = refs
    core = lax.axis_index("chan")
    at = 0
    copies = []
    for index, piece in enumerate(pieces):
        copies.append(
            pltpu.make_async_copy(rows.at[core, at : at + piece.shape[0], :], piece, sems.at[index])
        )
        at += piece.shape[0]
    wait_all(start_all(copies))


def in_hbm(array):
    return pltpu.with_memory_space_constraint(array, pltpu.HBM)


def limit(mebibytes):
    return pltpu.CompilerParams(vmem_limit_bytes=mebibytes * 1024 * 1024)


def cost(flops=1000):
    return pl.CostEstimate(flops=flops, bytes_accessed=1000, transcendentals=0)


def anywhere(count):
    return [pl.BlockSpec(memory_space=pl.ANY)] * count


def vmem(count):
    return [pl.BlockSpec(memory_space=pltpu.VMEM)] * count


def plans_of(cuts, lon_blocks, block_width, block_most):
    reach = block_most - 1
    plans = []
    first = 0
    for index in range(1, len(cuts)):
        last = cuts[index] - reach if index < len(cuts) - 1 else lon_blocks
        need = []
        for block in range(first, last + reach):
            block %= lon_blocks
            piece = max(which for which in range(len(cuts) - 1) if cuts[which] <= block)
            low = (block - cuts[piece]) * block_width
            if need and need[-1][0] == piece and need[-1][2] == low:
                need[-1][2] = low + block_width
            else:
                need.append([piece, low, low + block_width])
        plans.append(dict(
            first=first, places=last - first,
            pieces=[piece for piece, _, _ in need], spans=[(low, high) for _, low, high in need],
        ))
        first = last
    return plans


def per_device(
    state_in, basis_blocks, block_start, block_count, mix_weight, up_weight, down_weight
):
    bands = lax.axis_size("lat")
    local_rows, basis_count, block_width, taps, block_most = basis_blocks.shape[:5]
    cells, width = state_in.shape[1:]
    channels = mix_weight.shape[2]
    units = 2 * up_weight.shape[1]
    lon_blocks = cells // block_width
    depth = block_most * block_width
    filter_rows = basis_count * block_width
    swap = [(0, 1), (1, 0)]
    pairs = []
    for band in range(bands - 1):
        pairs += [(2 * band + 1, 2 * band + 2), (2 * band + 2, 2 * band + 1)]

    sizes = dict(block_width=block_width, lon_blocks=lon_blocks)
    smem = [pl.BlockSpec(memory_space=pltpu.SMEM)]
    narrow = state_in.dtype

    def row_pieces(cuts):
        return [pltpu.VMEM(((high - low) * block_width, width), narrow) for low, high in zip(cuts, cuts[1:])]

    edge = pl.pallas_call(
        edge_kernel,
        out_shape=row_pieces(FIRST_CUTS),
        in_specs=anywhere(1),
        out_specs=vmem(len(FIRST_CUTS) - 1),
        scratch_shapes=[pltpu.SemaphoreType.DMA((len(FIRST_CUTS) - 1,))],
        compiler_params=limit(4),
        cost_estimate=cost(),
        name="edge_row",
    )(in_hbm(state_in))
    halo_other = [lax.ppermute(piece, ("lat", "chan"), pairs) for piece in edge]
    other = lax.ppermute(state_in, "chan", swap)
    mix_other = lax.ppermute(mix_weight, "chan", swap)
    up_other = lax.ppermute(up_weight, "chan", swap)
    down_other = lax.ppermute(down_weight, "chan", swap)

    basis_flat = basis_blocks.reshape(local_rows * filter_rows * taps * block_most, block_width)
    mixing = (basis_count * width, channels)
    weights = (
        in_hbm(mix_weight.reshape(mixing)), mix_other.reshape(mixing),
        in_hbm(up_weight), up_other, in_hbm(down_weight), down_other,
    )
    conv_shape = jax.ShapeDtypeStruct((lon_blocks, filter_rows, width), jnp.float32)
    wide_window = pltpu.VMEM((cells + depth - block_width, channels), narrow)
    staged = [mixing, mixing, (channels, units), (units, channels)]
    conv_own, conv_other, residual, edge_filter, mix_own, mix_other, up, down = pl.pallas_call(
        functools.partial(local_kernel, block_most=block_most, **sizes),
        out_shape=[
            conv_shape, conv_shape, jax.ShapeDtypeStruct((cells, channels), jnp.float32),
            jax.ShapeDtypeStruct((filter_rows, depth), narrow),
            *[jax.ShapeDtypeStruct(shape, narrow) for shape in staged],
        ],
        in_specs=smem * 2 + anywhere(2) + vmem(1) + anywhere(len(weights)),
        out_specs=vmem(4 + len(staged)),
        scratch_shapes=[
            pltpu.VMEM(state_in.shape, narrow),
            pltpu.VMEM((basis_flat.shape[0] // local_rows, block_width), narrow),
            pltpu.VMEM((taps, filter_rows, depth), narrow),
            pltpu.VMEM((filter_rows, 2 * depth), narrow),
            wide_window, wide_window,
            pltpu.SemaphoreType.DMA, pltpu.SemaphoreType.DMA, pltpu.SemaphoreType.DMA((12,)),
        ],
        compiler_params=limit(16),
        cost_estimate=cost(),
        name="local_taps",
    )(block_start, block_count, in_hbm(basis_flat), in_hbm(state_in), other, *weights)

    relay = pl.pallas_call(
        relay_kernel,
        out_shape=row_pieces(LAST_CUTS),
        in_specs=vmem(1) + anywhere(1),
        out_specs=vmem(len(LAST_CUTS) - 1),
        compiler_params=limit(4),
        cost_estimate=cost(),
        name="relay_rows",
    )(other, edge_filter)
    halo_own = [lax.ppermute(piece, ("lat", "chan"), pairs) for piece in relay]

    def halo_scratch(plan):
        return [
            pltpu.VMEM(((plan["places"] + block_most - 1) * block_width, width), narrow),
            pltpu.VMEM((plan["places"] * block_width, basis_count * width), narrow),
        ]

    partials = []
    first_plans = plans_of(FIRST_CUTS, lon_blocks, block_width, block_most)
    for plan in first_plans:
        done = partials[-1:]
        partials.append(pl.pallas_call(
            functools.partial(
                first_half_kernel, plan=plan, ordered=len(done), block_width=block_width, rows=local_rows * bands
            ),
            out_shape=jax.ShapeDtypeStruct((plan["places"] * block_width, channels), jnp.float32),
            in_specs=vmem(len(plan["pieces"])) + anywhere(len(done)) + vmem(4),
            out_specs=vmem(1)[0],
            scratch_shapes=halo_scratch(plan),
            compiler_params=limit(10),
            cost_estimate=cost(6 * 10**10),
            name="edge_tap_first_half",
        )(*[halo_other[piece] for piece in plan["pieces"]], *done, edge_filter, conv_other, mix_other, residual))

    sends, done = {}, partials[-1:]
    last_plans = plans_of(LAST_CUTS, lon_blocks, block_width, block_most)
    firsts = (0, last_plans[-1]["first"])
    for plan in last_plans:
        low, high = plan["first"], plan["first"] + plan["places"]
        states, state_spans = [], []
        for partial, other_plan in zip(partials, first_plans):
            begin = max(low, other_plan["first"])
            end = min(high, other_plan["first"] + other_plan["places"])
            if begin < end:
                states.append(partial)
                state_spans.append((
                    (begin - other_plan["first"]) * block_width, (end - other_plan["first"]) * block_width
                ))
        plan["sent_from"] = max(place for place in firsts if place <= low)
        sent = (firsts[1] if plan["sent_from"] == 0 else lon_blocks) - plan["sent_from"]
        plan["all"] = max(plan["pieces"]) + 1
        aliases = {plan["all"] + index: index for index in range(len(done))} if low else {}
        used = [vmem(1) if piece in plan["pieces"] else anywhere(1) for piece in range(plan["all"])]
        keep, send = pl.pallas_call(
            functools.partial(
                tail_kernel, plan=plan, ordered=len(done), block_width=block_width, state_spans=state_spans,
                rows=local_rows * bands,
            ),
            out_shape=[jax.ShapeDtypeStruct((size, width), narrow) for size in (cells, sent * block_width)],
            in_specs=sum(used, []) + anywhere(len(done)) + vmem(len(states) + 5),
            out_specs=vmem(2),
            scratch_shapes=halo_scratch(plan),
            input_output_aliases=aliases,
            compiler_params=limit(14),
            cost_estimate=cost(10**10 if high == lon_blocks else 1000),
            name="edge_tap_and_feed",
        )(
            *halo_own[: plan["all"]], *done, *states,
            edge_filter, conv_own, mix_own, up, down,
        )
        sends[plan["sent_from"]] = send
        done = [keep] if high == firsts[1] else [keep, send]

    early = lax.ppermute(sends[0], "chan", swap)
    late, early = lax.optimization_barrier((sends[firsts[1]], early))
    late = lax.ppermute(late, "chan", swap)
    result = jax.ShapeDtypeStruct(state_in.shape, narrow)
    placed = pl.pallas_call(
        functools.partial(place_kernel, firsts=firsts[:-1], **sizes),
        out_shape=result,
        in_specs=vmem(len(firsts) + 1),
        out_specs=anywhere(1)[0],
        scratch_shapes=[pltpu.SemaphoreType.DMA((len(firsts),))],
        cost_estimate=cost(),
        compiler_params=limit(4),
        name="place_rows",
    )(block_start, keep, early)

    return pl.pallas_call(
        functools.partial(place_last_kernel, first=firsts[-1], **sizes),
        out_shape=result,
        in_specs=vmem(2) + anywhere(1),
        out_specs=anywhere(1)[0],
        scratch_shapes=[pltpu.SemaphoreType.DMA],
        input_output_aliases={2: 0},
        cost_estimate=cost(),
        compiler_params=limit(4),
        name="place_last_rows",
    )(block_start, late, placed)


def solution(mesh):
    placed = (
        P(("grp", "lat"), None, "chan"),
        P("lat", None, None, None, None, None),
        P("lat", None),
        P("lat", None),
        P(None, "chan", None),
        P(None, "chan"),
        P("chan", None),
    )
    return jax.shard_map(
        per_device,
        mesh=mesh,
        in_specs=placed,
        out_specs=P(("grp", "lat"), None, "chan"),
        check_vma=False,
    )
```

```python
import functools

import jax
import jax.numpy as jnp
from jax import lax
from jax.experimental import pallas as pl
from jax.experimental.pallas import tpu as pltpu
from jax.sharding import PartitionSpec as P

GROUP = 9
TILE = 16
FIRST_CUTS = (0, 18)
LAST_CUTS = (0, 8, 13, 18)


def start_all(copies):
    for copy in copies:
        copy.start()
    return copies


def wait_all(copies):
    for copy in copies:
        copy.wait()


def halo_start(block_start, core):
    return block_start[core, 2 * core]


def block_rows(block, block_width, blocks=1):
    return pl.ds(pl.multiple_of(block * block_width, block_width), blocks * block_width)


def wrap(block, lon_blocks):
    return jnp.where(block >= lon_blocks, block - lon_blocks, block)


def home_block(place, start, lon_blocks):
    return jnp.where(place < start, place + lon_blocks - start, place - start)


def spread_filters(basis, counts, core, filters, block_most):
    rows_out, taps, width = filters.shape[1], filters.shape[0], basis.shape[1]
    pieces = taps * block_most
    size = TILE * pieces
    row = lax.broadcasted_iota(jnp.int32, (size, size), 0)
    column = lax.broadcasted_iota(jnp.int32, (size, size), 1)
    order = (column == lax.rem(row, TILE) * pieces + row // TILE).astype(jnp.float32).astype(jnp.bfloat16)
    for tile in range(rows_out // TILE):
        sorted_rows = jnp.dot(
            order, basis[tile * size : (tile + 1) * size, :], preferred_element_type=jnp.float32
        ).astype(jnp.bfloat16)
        for tap in range(taps):
            for block in range(block_most):
                at = (tap * block_most + block) * TILE
                piece = sorted_rows[at : at + TILE]
                filters[tap, tile * TILE : (tile + 1) * TILE, block * width : (block + 1) * width] = (
                    jnp.where(block < counts[core, tap], piece, jnp.zeros_like(piece))
                )


def stage_weights(core, sources, targets, sem, width):
    (mix, mix_other, up, up_other, down, down_other) = sources
    (mix_to, mix_other_to, up_to, down_to) = targets
    pairs = []
    for place, half in enumerate((core, 1 - core)):
        theirs = pl.ds(pl.multiple_of(half * width, width), width)
        ours = slice(place * width, (place + 1) * width)
        pairs += [(mix.at[:, theirs], mix_to.at[:, ours]), (mix_other.at[:, theirs], mix_other_to.at[:, ours])]
        for index, (rows, columns) in enumerate(((up, down), (up_other, down_other))):
            units = slice(index * rows.shape[1], (index + 1) * rows.shape[1])
            pairs += [
                (rows.at[theirs, :], up_to.at[ours, units]),
                (columns.at[:, theirs], down_to.at[units, ours]),
            ]
    return [pltpu.make_async_copy(source, target, sem.at[index]) for index, (source, target) in enumerate(pairs)]


def local_kernel(
    block_start, block_count, basis_from, own_from, other, *refs, lon_blocks, block_width, block_most
):
    sources, refs = refs[:6], refs[6:]
    conv_own, conv_other, residual, edge_filter, *targets = refs[:8]
    own, basis, filters, near, window0, window1, own_sem, basis_sem, weight_sems = refs[8:]
    core = lax.axis_index("chan")
    cells, width = own.shape[1:]
    depth = block_most * block_width
    rows = basis.shape[0]
    first_copies = start_all([
        pltpu.make_async_copy(
            basis_from.at[pl.ds(pl.multiple_of(core * rows, rows), rows), :], basis, basis_sem
        ),
        pltpu.make_async_copy(own_from, own, own_sem),
    ])
    weight_copies = start_all(stage_weights(core, sources, targets, weight_sems, width))
    start = halo_start(block_start, core)
    fills = ((0, other), (1, own))
    for which, (half, source) in enumerate(fills):
        lanes = slice((1 - half) * width, (2 - half) * width)
        if which == 1:
            wait_all(first_copies)
        for row, window in enumerate((window0, window1)):
            window[:cells, lanes] = source[row]
            window[cells:, lanes] = source[row, : window.shape[0] - cells]
        for place in range(lon_blocks):
            home = block_rows(home_block(place, start, lon_blocks), block_width)
            residual[place * block_width : (place + 1) * block_width, lanes] = (
                source[core, home, :].astype(jnp.float32)
            )
    spread_filters(basis, block_count, core, filters, block_most)
    near[:, :depth] = filters[1 - core]
    near[:, depth:] = filters[2 - core]
    edge_filter[...] = filters[2 * core]
    starts = (block_start[core, 1 - core], block_start[core, 2 - core])

    def group_step(group, carry):
        for slot in range(GROUP):
            place = group * GROUP + slot
            home = home_block(place, start, lon_blocks)
            parts = []
            for window, tap_start in zip((window0, window1), starts):
                source = wrap(home + tap_start, lon_blocks)
                parts.append(window[block_rows(source, block_width, block_most), :])
            result = jnp.dot(near[...], jnp.concatenate(parts, axis=0), preferred_element_type=jnp.float32)
            conv_own[place] = result[:, :width]
            conv_other[place] = result[:, width:]
        return carry

    lax.fori_loop(0, lon_blocks // GROUP, group_step, 0)
    wait_all(weight_copies)


def by_count(rows, filters, block_width, body):
    depth = filters.shape[1]
    row = rows // lax.axis_size("lat") * lax.axis_index("lat") + lax.axis_index("chan")
    few = 3 * (rows - row) * (rows - row) < 2 * rows * rows
    short = min(depth, -(-(depth - block_width) // 128) * 128)
    pl.when(few)(lambda: body(short))
    pl.when(jnp.logical_not(few))(lambda: body(depth))


def halo_mix(depth, first, places, block_width, halves, spans, edge_filter, conv_local, mix, window, conv):
    at = 0
    for half, (low, high) in zip(halves, spans):
        window[at : at + high - low, :] = half[low:high, :]
        at += high - low
    width = window.shape[1]
    for slot in range(places):
        result = conv_local[first + slot] + jnp.dot(
            edge_filter[:, :depth], window[slot * block_width : slot * block_width + depth, :],
            preferred_element_type=jnp.float32,
        )
        rounded = result.astype(jnp.bfloat16)
        for basis in range(edge_filter.shape[0] // block_width):
            conv[
                slot * block_width : (slot + 1) * block_width, basis * width : (basis + 1) * width
            ] = rounded[basis * block_width : (basis + 1) * block_width]
    return jnp.dot(conv[...], mix[...], preferred_element_type=jnp.float32)


def window_kernel(half, window):
    cells = half.shape[0]
    window[:cells, :] = half[...]
    window[cells:, :] = half[: window.shape[0] - cells, :]


def first_half_kernel(
    window, edge_filter, conv_local, mix, residual, result, conv, *, plan, block_width, rows
):
    first, places = plan["first"], plan["places"]

    def body(depth):
        mixed = halo_mix(
            depth, first, places, block_width, (), (), edge_filter, conv_local, mix, window, conv
        )
        result[...] = residual[first * block_width : (first + places) * block_width, :] + mixed

    by_count(rows, edge_filter, block_width, body)


def gelu(x):
    return 0.5 * x * (1.0 + lax.erf(x * 0.7071067811865476))


def tail_kernel(*refs, plan, ordered, block_width, state_spans, rows):
    count = plan["all"]
    halves, refs = [refs[piece] for piece in plan["pieces"]], refs[count + ordered :]
    partials, refs = refs[: len(state_spans)], refs[len(state_spans) :]
    edge_filter, conv_local, mix, up, down, keep, send, window, conv = refs

    def body(depth):
        mixed = halo_mix(
            depth, plan["first"], plan["places"], block_width, halves, plan["spans"], edge_filter, conv_local, mix,
            window, conv,
        )
        before = [partial[low:high, :] for partial, (low, high) in zip(partials, state_spans)]
        state = mixed + (before[0] if len(before) == 1 else jnp.concatenate(before, axis=0))
        width = send.shape[1]
        hidden = gelu(
            jnp.dot(state.astype(jnp.bfloat16), up[...], preferred_element_type=jnp.float32)
        ).astype(jnp.bfloat16)
        total = state + jnp.dot(hidden, down[...], preferred_element_type=jnp.float32)
        total = total.astype(jnp.bfloat16)
        first = plan["first"] * block_width
        keep[first : first + total.shape[0], :] = total[:, :width]
        first -= plan["sent_from"] * block_width
        send[first : first + total.shape[0], :] = total[:, width:]

    by_count(rows, edge_filter, block_width, body)


def begin_place(source, result, row, home, sem, lon_blocks, block_width):
    places = source.shape[0] // block_width

    def begin(count):
        size = count * block_width
        pltpu.make_async_copy(
            source.at[:size, :], result.at[row, block_rows(home, block_width, count), :], sem
        ).start()
        if count < places:
            pltpu.make_async_copy(
                source.at[size:, :], result.at[row, : source.shape[0] - size, :], sem
            ).start()

    def choose(low, high):
        if low == high:
            begin(low)
            return
        middle = (low + high) // 2
        early = lon_blocks - home <= middle
        pl.when(early)(lambda: choose(low, middle))
        pl.when(jnp.logical_not(early))(lambda: choose(middle + 1, high))

    choose(1, places)
    return pltpu.make_async_copy(source, result.at[row, : source.shape[0], :], sem)


def scalar_start(block_start, row):
    shape = block_start.shape
    here = jnp.logical_and(
        lax.broadcasted_iota(jnp.int32, shape, 0) == row, lax.broadcasted_iota(jnp.int32, shape, 1) == 2 * row
    )
    return jnp.max(jnp.where(here, block_start[...].astype(jnp.float32), 0.0)).astype(jnp.int32)


def place_kernel(block_start, keep, *refs, firsts, lon_blocks, block_width):
    *received, result, sems = refs
    core = lax.axis_index("chan")
    waits = []
    for index, (source, first) in enumerate(zip((keep, *received), (0, *firsts))):
        row = 1 - core if index else core
        if index < 2:
            start = scalar_start(block_start, row)
        waits.append(begin_place(
            source, result, row, home_block(first, start, lon_blocks), sems.at[index], lon_blocks, block_width
        ))
    wait_all(waits)


def place_last_kernel(block_start, source, before, result, sem, *, first, lon_blocks, block_width):
    row = 1 - lax.axis_index("chan")
    home = home_block(first, scalar_start(block_start, row), lon_blocks)
    begin_place(source, result, row, home, sem, lon_blocks, block_width).wait()


def relay_kernel(other, ordered, *pieces):
    core = lax.axis_index("chan")
    at = 0
    for piece in pieces:
        piece[...] = other[core, at : at + piece.shape[0], :]
        at += piece.shape[0]


def edge_kernel(rows, *refs):
    *pieces, sems = refs
    core = lax.axis_index("chan")
    at = 0
    copies = []
    for index, piece in enumerate(pieces):
        copies.append(
            pltpu.make_async_copy(rows.at[core, at : at + piece.shape[0], :], piece, sems.at[index])
        )
        at += piece.shape[0]
    wait_all(start_all(copies))


def in_hbm(array):
    return pltpu.with_memory_space_constraint(array, pltpu.HBM)


def limit(mebibytes):
    return pltpu.CompilerParams(vmem_limit_bytes=mebibytes * 1024 * 1024)


def cost(flops=1000):
    return pl.CostEstimate(flops=flops, bytes_accessed=1000, transcendentals=0)


def anywhere(count):
    return [pl.BlockSpec(memory_space=pl.ANY)] * count


def vmem(count):
    return [pl.BlockSpec(memory_space=pltpu.VMEM)] * count


def plans_of(cuts, lon_blocks, block_width, block_most):
    reach = block_most - 1
    plans = []
    first = 0
    for index in range(1, len(cuts)):
        last = cuts[index] - reach if index < len(cuts) - 1 else lon_blocks
        need = []
        for block in range(first, last + reach):
            block %= lon_blocks
            piece = max(which for which in range(len(cuts) - 1) if cuts[which] <= block)
            low = (block - cuts[piece]) * block_width
            if need and need[-1][0] == piece and need[-1][2] == low:
                need[-1][2] = low + block_width
            else:
                need.append([piece, low, low + block_width])
        plans.append(dict(
            first=first, places=last - first,
            pieces=[piece for piece, _, _ in need], spans=[(low, high) for _, low, high in need],
        ))
        first = last
    return plans


def per_device(
    state_in, basis_blocks, block_start, block_count, mix_weight, up_weight, down_weight
):
    bands = lax.axis_size("lat")
    local_rows, basis_count, block_width, taps, block_most = basis_blocks.shape[:5]
    cells, width = state_in.shape[1:]
    channels = mix_weight.shape[2]
    units = 2 * up_weight.shape[1]
    lon_blocks = cells // block_width
    depth = block_most * block_width
    filter_rows = basis_count * block_width
    swap = [(0, 1), (1, 0)]
    pairs = []
    for band in range(bands - 1):
        pairs += [(2 * band + 1, 2 * band + 2), (2 * band + 2, 2 * band + 1)]

    sizes = dict(block_width=block_width, lon_blocks=lon_blocks)
    smem = [pl.BlockSpec(memory_space=pltpu.SMEM)]
    narrow = state_in.dtype

    def row_pieces(cuts):
        return [pltpu.VMEM(((high - low) * block_width, width), narrow) for low, high in zip(cuts, cuts[1:])]

    edge = pl.pallas_call(
        edge_kernel,
        out_shape=row_pieces(FIRST_CUTS),
        in_specs=anywhere(1),
        out_specs=vmem(len(FIRST_CUTS) - 1),
        scratch_shapes=[pltpu.SemaphoreType.DMA((len(FIRST_CUTS) - 1,))],
        compiler_params=limit(4),
        cost_estimate=cost(),
        name="edge_row",
    )(in_hbm(state_in))
    halo_other = [lax.ppermute(piece, ("lat", "chan"), pairs) for piece in edge]
    other = lax.ppermute(state_in, "chan", swap)
    mix_other = lax.ppermute(mix_weight, "chan", swap)
    up_other = lax.ppermute(up_weight, "chan", swap)
    down_other = lax.ppermute(down_weight, "chan", swap)

    basis_flat = basis_blocks.reshape(local_rows * filter_rows * taps * block_most, block_width)
    mixing = (basis_count * width, channels)
    weights = (
        in_hbm(mix_weight.reshape(mixing)), mix_other.reshape(mixing),
        in_hbm(up_weight), up_other, in_hbm(down_weight), down_other,
    )
    conv_shape = jax.ShapeDtypeStruct((lon_blocks, filter_rows, width), jnp.float32)
    wide_window = pltpu.VMEM((cells + depth - block_width, channels), narrow)
    staged = [mixing, mixing, (channels, units), (units, channels)]
    conv_own, conv_other, residual, edge_filter, mix_own, mix_other, up, down = pl.pallas_call(
        functools.partial(local_kernel, block_most=block_most, **sizes),
        out_shape=[
            conv_shape, conv_shape, jax.ShapeDtypeStruct((cells, channels), jnp.float32),
            jax.ShapeDtypeStruct((filter_rows, depth), narrow),
            *[jax.ShapeDtypeStruct(shape, narrow) for shape in staged],
        ],
        in_specs=smem * 2 + anywhere(2) + vmem(1) + anywhere(len(weights)),
        out_specs=vmem(4 + len(staged)),
        scratch_shapes=[
            pltpu.VMEM(state_in.shape, narrow),
            pltpu.VMEM((basis_flat.shape[0] // local_rows, block_width), narrow),
            pltpu.VMEM((taps, filter_rows, depth), narrow),
            pltpu.VMEM((filter_rows, 2 * depth), narrow),
            wide_window, wide_window,
            pltpu.SemaphoreType.DMA, pltpu.SemaphoreType.DMA, pltpu.SemaphoreType.DMA((12,)),
        ],
        compiler_params=limit(16),
        cost_estimate=cost(),
        name="local_taps",
    )(block_start, block_count, in_hbm(basis_flat), in_hbm(state_in), other, *weights)

    relay = pl.pallas_call(
        relay_kernel,
        out_shape=row_pieces(LAST_CUTS),
        in_specs=vmem(1) + anywhere(1),
        out_specs=vmem(len(LAST_CUTS) - 1),
        compiler_params=limit(4),
        cost_estimate=cost(),
        name="relay_rows",
    )(other, edge_filter)
    halo_own = [lax.ppermute(piece, ("lat", "chan"), pairs) for piece in relay]

    def halo_scratch(plan):
        return [
            pltpu.VMEM(((plan["places"] + block_most - 1) * block_width, width), narrow),
            pltpu.VMEM((plan["places"] * block_width, basis_count * width), narrow),
        ]

    partials = []
    first_plans = plans_of(FIRST_CUTS, lon_blocks, block_width, block_most)
    window, conv = halo_scratch(first_plans[0])
    halo_window = pl.pallas_call(
        window_kernel,
        out_shape=jax.ShapeDtypeStruct(window.shape, narrow),
        in_specs=vmem(1),
        out_specs=vmem(1)[0],
        compiler_params=limit(4),
        cost_estimate=cost(6 * 10**10),
        name="halo_window",
    )(halo_other[0])
    partials.append(pl.pallas_call(
        functools.partial(
            first_half_kernel, plan=first_plans[0], block_width=block_width, rows=local_rows * bands
        ),
        out_shape=jax.ShapeDtypeStruct((cells, channels), jnp.float32),
        in_specs=vmem(5),
        out_specs=vmem(1)[0],
        scratch_shapes=[conv],
        compiler_params=limit(10),
        cost_estimate=cost(),
        name="edge_tap_first_half",
    )(halo_window, edge_filter, conv_other, mix_other, residual))

    sends, done = {}, partials[-1:]
    last_plans = plans_of(LAST_CUTS, lon_blocks, block_width, block_most)
    firsts = (0, last_plans[-1]["first"])
    for plan in last_plans:
        low, high = plan["first"], plan["first"] + plan["places"]
        states, state_spans = [], []
        for partial, other_plan in zip(partials, first_plans):
            begin = max(low, other_plan["first"])
            end = min(high, other_plan["first"] + other_plan["places"])
            if begin < end:
                states.append(partial)
                state_spans.append((
                    (begin - other_plan["first"]) * block_width, (end - other_plan["first"]) * block_width
                ))
        plan["sent_from"] = max(place for place in firsts if place <= low)
        sent = (firsts[1] if plan["sent_from"] == 0 else lon_blocks) - plan["sent_from"]
        plan["all"] = max(plan["pieces"]) + 1
        aliases = {plan["all"] + index: index for index in range(len(done))} if low else {}
        used = [vmem(1) if piece in plan["pieces"] else anywhere(1) for piece in range(plan["all"])]
        keep, send = pl.pallas_call(
            functools.partial(
                tail_kernel, plan=plan, ordered=len(done), block_width=block_width, state_spans=state_spans,
                rows=local_rows * bands,
            ),
            out_shape=[jax.ShapeDtypeStruct((size, width), narrow) for size in (cells, sent * block_width)],
            in_specs=sum(used, []) + anywhere(len(done)) + vmem(len(states) + 5),
            out_specs=vmem(2),
            scratch_shapes=halo_scratch(plan),
            input_output_aliases=aliases,
            compiler_params=limit(14),
            cost_estimate=cost(10**10 if high == lon_blocks else 1000),
            name="edge_tap_and_feed",
        )(
            *halo_own[: plan["all"]], *done, *states,
            edge_filter, conv_own, mix_own, up, down,
        )
        sends[plan["sent_from"]] = send
        done = [keep] if high == firsts[1] else [keep, send]

    early = lax.ppermute(sends[0], "chan", swap)
    late, early = lax.optimization_barrier((sends[firsts[1]], early))
    late = lax.ppermute(late, "chan", swap)
    result = jax.ShapeDtypeStruct(state_in.shape, narrow)
    placed = pl.pallas_call(
        functools.partial(place_kernel, firsts=firsts[:-1], **sizes),
        out_shape=result,
        in_specs=vmem(len(firsts) + 1),
        out_specs=anywhere(1)[0],
        scratch_shapes=[pltpu.SemaphoreType.DMA((len(firsts),))],
        cost_estimate=cost(),
        compiler_params=limit(4),
        name="place_rows",
    )(block_start, keep, early)

    return pl.pallas_call(
        functools.partial(place_last_kernel, first=firsts[-1], **sizes),
        out_shape=result,
        in_specs=vmem(2) + anywhere(1),
        out_specs=anywhere(1)[0],
        scratch_shapes=[pltpu.SemaphoreType.DMA],
        input_output_aliases={2: 0},
        cost_estimate=cost(),
        compiler_params=limit(4),
        name="place_last_rows",
    )(block_start, late, placed)


def solution(mesh):
    placed = (
        P(("grp", "lat"), None, "chan"),
        P("lat", None, None, None, None, None),
        P("lat", None),
        P("lat", None),
        P(None, "chan", None),
        P(None, "chan"),
        P("chan", None),
    )
    return jax.shard_map(
        per_device,
        mesh=mesh,
        in_specs=placed,
        out_specs=P(("grp", "lat"), None, "chan"),
        check_vma=False,
    )
```
